32 devices in a mesh: gz: 4 (over y, x), xy: 8 (over z, core).
Axes of the slice: x: 2, y: 2, z: 4, core: 2. Of those that a mesh axis runs over, the one named last changes fastest.
Arguments:
- solution: float32 [16, 1536, 1536], P('gz', 'xy'), may hold values from -6 to 6
- residual: float32 [16, 1536, 1536], P('gz', 'xy'), may hold values from -14 to 14
- direction: float32 [16, 1536, 1536], P('gz', 'xy'), may hold values from -14 to 14
- volume_fraction: float32 [16, 1536, 1536], P('gz', 'xy'), may hold values from 0 to 1, as said below
- density: float32 [2], replicated, may hold values from 0.08 to 1.25, as said below
Outputs:
- new_solution: float32 [16, 1536, 1536], P('gz', 'xy')
- new_residual: float32 [16, 1536, 1536], P('gz', 'xy')
- new_direction: float32 [16, 1536, 1536], P('gz', 'xy')
The draws below stay inside these ranges and needn't reach their ends.
Inputs may be any that keep to these rules, and one draw needn't show every extreme that they name: `volume_fraction`: 0 marks a cell filled with liquid and 1 a cell filled with gas; cells in between hold both. Entry 0 is the liquid's density and entry 1 the gas's.
All inputs are finite; a program needn't handle non-finite values.
Results may differ from the reference program's by a relative error of at most 0.0003.
Values sent between devices are 32-bit elements; how exact they have to be, the bound alone decides.
No kernel may reach another device: no remote copies, remote signals or barrier semaphores. Data moves between devices by JAX's collectives and lax.ppermute only.
A program may use at most 128 MiB of HBM per device.

```python
import jax
import jax.numpy as jnp
from jax import lax

NX = 1536
NY = 1536
NZ = 16


def shared_field(key):
    levels = jnp.arange(NZ, dtype=jnp.float32)[:, None, None] / NZ
    columns = jnp.arange(NX, dtype=jnp.float32)[None, :, None] / NX
    profile = jnp.exp(0.55 * jnp.log(3.0) * (levels + columns))
    noise_field = jax.random.truncated_normal(key, -4.0, 4.0, (NZ, NX, NY), jnp.float32)
    return noise_field * profile


def draw_residual(key, part):
    return shared_field(jax.random.fold_in(key, 11))


def draw_direction(key, part):
    common = shared_field(jax.random.fold_in(key, 11))
    own_noise = jax.random.truncated_normal(jax.random.fold_in(key, 23), -4.0, 4.0, (NZ, NX, NY), jnp.float32)
    return 0.8 * common + 0.6 * own_noise


def draw_volume_fraction(key, part):
    subkeys = jax.random.split(jax.random.fold_in(key, 37), 7)
    steepness = jax.random.uniform(subkeys[0], (), jnp.float32, 0.5 * NZ, 1.0 * NZ)
    slope_sign = 2.0 * jax.random.randint(subkeys[1], (), 0, 2).astype(jnp.float32) - 1.0
    cross_tilt = jax.random.uniform(subkeys[2], (), jnp.float32, -0.25 * NZ, 0.25 * NZ)
    column_pos = (2.0 * jnp.arange(NX, dtype=jnp.float32)[:, None] - NX + 1.0) / (2.0 * NX)
    row_pos = (2.0 * jnp.arange(NY, dtype=jnp.float32)[None, :] - NY + 1.0) / (2.0 * NY)
    height = 0.5 * NZ + slope_sign * steepness * column_pos + cross_tilt * row_pos
    height = height + jax.random.uniform(subkeys[3], (NX, NY), jnp.float32, -1.0, 1.0)
    smear = jax.random.uniform(subkeys[4], (NX, NY), jnp.float32, 2.0, 3.0)
    levels = jnp.arange(NZ, dtype=jnp.float32)[:, None, None] + 0.5
    fraction = jnp.clip((levels - height[None]) / smear[None] + 0.5, 0.0, 1.0)
    dispersed = jax.random.randint(subkeys[5], (NZ, NX, NY), 0, 4) == 0
    droplet = jax.random.uniform(subkeys[6], (NZ, NX, NY), jnp.float32, 0.0, 1.0)
    return jnp.where(dispersed, droplet, fraction)


def draw_density(key, part):
    subkeys = jax.random.split(jax.random.fold_in(key, 53), 2)
    liquid = jax.random.uniform(subkeys[0], (), jnp.float32, 0.8, 1.25)
    vapour = jax.random.uniform(subkeys[1], (), jnp.float32, 0.08, 0.3)
    return jnp.stack([liquid, vapour])


def block_scale(own_key, extent, pieces, low, largest):
    factor_of = 1.0
    for dim, blocks in pieces:
        heights = jax.random.uniform(jax.random.fold_in(jax.random.fold_in(own_key, 6), dim), (blocks,), jnp.float32, low / len(pieces), largest / len(pieces))
        factor_of = factor_of * jnp.repeat(jnp.exp(heights), extent[dim] // blocks).reshape((-1,) + (1,) * (len(extent) - 1 - dim))
    return factor_of


def gaussian(stream_key, extent, deviation, bound, pieces=(), kind=jnp.bfloat16):
    array = deviation * jax.random.normal(stream_key, extent, jnp.float32)
    if pieces:
        array = array * block_scale(stream_key, extent, pieces, -0.22, 0.18)
    return jnp.clip(array, -bound, bound).astype(kind)


def setup_inputs(seed: int = 0) -> dict:
    arg_keys = jax.random.split(jax.random.key(seed), 6)
    solution = gaussian(arg_keys[0], (NZ, NX, NY), 1.0, 6.0, ((0, 4), (1, 8)), jnp.float32)
    residual = draw_residual(jax.random.fold_in(arg_keys[5], 71), 0)
    direction = draw_direction(jax.random.fold_in(arg_keys[5], 71), 0)
    volume_fraction = draw_volume_fraction(jax.random.fold_in(arg_keys[5], 71), 0)
    density = draw_density(jax.random.fold_in(arg_keys[5], 71), 0)
    return {"solution": solution, "residual": residual, "direction": direction, "volume_fraction": volume_fraction, "density": density}


HIGHEST_PRECISION = lax.Precision.HIGHEST

def cosine_table(length):
    freq_ids = jnp.arange(length, dtype=jnp.int32)[:, None]
    cell_ids = jnp.arange(length, dtype=jnp.int32)[None, :]
    phase_ids = freq_ids * (2 * cell_ids + 1) % (4 * length)
    angles = jnp.pi / (2 * length) * phase_ids.astype(jnp.float32)
    weights = jnp.where(freq_ids == 0, jnp.sqrt(1.0 / length), jnp.sqrt(2.0 / length)).astype(jnp.float32)
    return weights * jnp.cos(angles)

def eigenvalues(length):
    halves = jnp.sin(jnp.pi / (2 * length) * jnp.arange(length, dtype=jnp.int32).astype(jnp.float32))
    return 4.0 * halves * halves

def level_rows(height, total_depth, stiffness, spectrum):
    nothing = 0.0 * stiffness
    subdiagonal_entries = jnp.where(height > 0, -stiffness, nothing)
    super_diag = jnp.where(height < total_depth - 1, -stiffness, nothing)
    main_diag = stiffness * spectrum + jnp.where(height > 0, stiffness, nothing) + jnp.where(height < total_depth - 1, stiffness, 2.0 * stiffness)
    return (subdiagonal_entries, main_diag, super_diag)

def tridiagonal_solve(source_terms, column_heights, total_depth, stiffness, spectrum):

    def forward_pass(carried_state, step_element):
        ratio_before, elimination_before = carried_state
        source_term, height = step_element
        subdiagonal_entries, main_diag, super_diag = level_rows(height, total_depth, stiffness, spectrum)
        pivot_current = main_diag - subdiagonal_entries * ratio_before
        ratio_current = super_diag / pivot_current
        elimination_current = (source_term - subdiagonal_entries * elimination_before) / pivot_current
        return ((ratio_current, elimination_current), (ratio_current, elimination_current))
    initial_state = (jnp.zeros_like(spectrum), jnp.zeros_like(source_terms[0]))
    unused_slot, (ratio_values, elimination_values) = lax.scan(forward_pass, initial_state, (source_terms, column_heights))

    def backward_pass(value_following, step_element):
        ratio_current, elimination_current = step_element
        value_current = elimination_current - ratio_current * value_following
        return (value_current, value_current)
    unused_slot, solved_values = lax.scan(backward_pass, jnp.zeros_like(source_terms[0]), (ratio_values, elimination_values), reverse=True)
    return solved_values

def apply_operator(values, density_field):
    padded = jnp.pad(values, 1)
    dense_pad = jnp.pad(density_field, 1)
    shape_all = values.shape
    level_ids = lax.broadcasted_iota(jnp.int32, shape_all, 0)
    column_ids = lax.broadcasted_iota(jnp.int32, shape_all, 1)
    row_ids = lax.broadcasted_iota(jnp.int32, shape_all, 2)
    pairs = [(padded[2:, 1:-1, 1:-1], dense_pad[2:, 1:-1, 1:-1], level_ids >= 0), (padded[:-2, 1:-1, 1:-1], dense_pad[:-2, 1:-1, 1:-1], level_ids > 0), (padded[1:-1, 2:, 1:-1], dense_pad[1:-1, 2:, 1:-1], column_ids < shape_all[1] - 1), (padded[1:-1, :-2, 1:-1], dense_pad[1:-1, :-2, 1:-1], column_ids > 0), (padded[1:-1, 1:-1, 2:], dense_pad[1:-1, 1:-1, 2:], row_ids < shape_all[2] - 1), (padded[1:-1, 1:-1, :-2], dense_pad[1:-1, 1:-1, :-2], row_ids > 0)]
    result = jnp.zeros(shape_all, jnp.float32)
    for neighbour, dense_next, inside in pairs:
        result = result + jnp.where(inside, 2.0 / (density_field + dense_next) * (values - neighbour), 0.0)
    return result

def precondition(source_field, stiffness):
    total_depth, total_width, span_len = source_field.shape
    table_x = cosine_table(total_width)
    table_y = cosine_table(span_len)
    along_y = jnp.einsum('zxy,ky->zxk', source_field, table_y, precision=HIGHEST_PRECISION)
    spectral = jnp.einsum('zxk,jx->zkj', along_y, table_x, precision=HIGHEST_PRECISION)
    spectrum = eigenvalues(span_len)[:, None] + eigenvalues(total_width)[None, :]
    column_heights = jnp.arange(total_depth, dtype=jnp.int32)
    solved_values = tridiagonal_solve(spectral, column_heights, total_depth, stiffness, spectrum)
    back_x = jnp.einsum('zkj,jx->zkx', solved_values, table_x, precision=HIGHEST_PRECISION)
    return jnp.einsum('zkx,ky->zxy', back_x, table_y, precision=HIGHEST_PRECISION)

def reference(solution, residual, direction, volume_fraction, density):
    density_field = volume_fraction * density[1] + (1.0 - volume_fraction) * density[0]
    stiffness = 0.5 * (1.0 / density[0] + 1.0 / density[1])
    image_old = apply_operator(direction, density_field)
    precond = precondition(residual, stiffness)
    image_new = apply_operator(precond, density_field)
    total_zero = jnp.sum(direction * image_old)
    total_one = jnp.sum(precond * image_old)
    total_two = jnp.sum(residual * precond)
    total_three = jnp.sum(residual * direction)
    total_four = jnp.sum(precond * image_new)
    total_five = jnp.sum(direction * image_new)
    conjugate = -total_one / total_zero
    along_r = total_two + conjugate * total_three
    curvature = total_four + conjugate * (total_one + total_five) + conjugate * conjugate * total_zero
    step_len = along_r / curvature
    new_direction = precond + conjugate * direction
    new_solution = solution + step_len * new_direction
    new_residual = residual - step_len * (image_new + conjugate * image_old)
    return (new_solution, new_residual, new_direction)
```

```python
import functools

import jax
import jax.numpy as jnp
import numpy as np
from jax import lax
from jax.experimental import pallas as pl
from jax.experimental.pallas import tpu as pltpu
from jax.sharding import PartitionSpec as P

F32 = jnp.float32
BF16 = jnp.bfloat16
MIB = 1024 * 1024


def divisor_of(length, unit, largest):
    return max(t for t in range(unit, largest + 1, unit) if length % t == 0)


def halves_of(table):
    high = table.astype(BF16)
    low = (table - high.astype(np.float64)).astype(BF16)
    return high, low


def split(values):
    high = values.astype(BF16)
    return high, (values - high.astype(F32)).astype(BF16)


def dot(a, b):
    return jnp.dot(a, b, preferred_element_type=F32)


def dot3(a_high, a_low, b_high, b_low):
    return dot(a_high, b_high) + (dot(a_low, b_high) + dot(a_high, b_low))


def cosine_table(length):
    freq = np.arange(length)[:, None]
    cell = np.arange(length)[None, :]
    angles = np.pi / (2 * length) * (freq * (2 * cell + 1) % (4 * length))
    return np.where(freq == 0, np.sqrt(1.0 / length), np.sqrt(2.0 / length)) * np.cos(angles)


def spectral_order(length):
    return np.concatenate([np.arange(0, length, 2), np.arange(1, length, 2)])


def half_tables(length):
    half = length // 2
    return cosine_table(length)[spectral_order(length), :half].reshape(2, half, half)


def eigenvalues(length):
    return 4.0 * np.sin(np.pi * np.arange(length) / (2 * length)) ** 2


def level_table(depth):
    modes = np.arange(depth)[:, None]
    levels = np.arange(depth)[None, :]
    return np.sqrt(2.0 / depth) * np.cos(np.pi * (2 * modes + 1) * (2 * levels + 1) / (4 * depth))


def decay_table(length, depth):
    mu = eigenvalues(length)[spectral_order(length)]
    lam = 4.0 * np.sin(np.pi * (2 * np.arange(depth) + 1) / (4 * depth)) ** 2
    excess = lam[:, None] + mu[None, :]
    return (1.0 + excess / 2 - np.sqrt(excess + excess * excess / 4)).astype(np.float32)


def flip_matrix(size):
    return np.eye(size)[::-1].astype(BF16)


def flipped(high, low, flip):
    size = flip.shape[0]
    count = high.shape[1] // size
    blocks = []
    for i in range(count):
        part = slice((count - 1 - i) * size, (count - i) * size)
        blocks.append(dot(high[:, part], flip) + dot(low[:, part], flip))
    return jnp.concatenate(blocks, axis=1)


def power(base, exponent):
    result = None
    while exponent:
        if exponent & 1:
            result = base if result is None else result * base
        base = base * base
        exponent >>= 1
    return result


def fixed(shape):
    return pl.BlockSpec(shape, lambda *_: (0,) * len(shape))


def in_hbm(array):
    return pltpu.with_memory_space_constraint(array, pltpu.HBM)


def hbm(shape):
    return pltpu.HBM(shape, F32)


def params(mib=24):
    return pltpu.CompilerParams(vmem_limit_bytes=mib * MIB)


def cost(flops, count):
    return pl.CostEstimate(flops=int(flops) // 16, bytes_accessed=int(count) // 4, transcendentals=0)


def forward_kernel(scale_ref, rows_ref, high_ref, low_ref, flip_ref, out_ref):
    half = rows_ref.shape[1] // 2
    first, second = rows_ref[:, :half], rows_ref[:, half:]
    mirror = flipped(*split(second), flip_ref[...])
    scale = scale_ref[0]
    for parity, folded in enumerate((first + mirror, first - mirror)):
        out = dot3(*split(folded), high_ref[parity], low_ref[parity])
        out_ref[:, parity * half : (parity + 1) * half] = scale * out


def flip_of(half):
    return flip_matrix(256 if half % 256 == 0 else 128)


def forward_rows(rows, scale):
    count, length = rows.shape
    half = length // 2
    tile = divisor_of(count, 8, 256)
    high, low = halves_of(half_tables(length).transpose(0, 2, 1))
    flip = flip_of(half)
    return pl.pallas_call(
        forward_kernel,
        grid=(count // tile,),
        in_specs=[
            pl.BlockSpec(memory_space=pltpu.SMEM),
            pl.BlockSpec((tile, length), lambda i: (i, 0)),
            fixed(high.shape),
            fixed(low.shape),
            fixed(flip.shape),
        ],
        out_specs=pl.BlockSpec((tile, length), lambda i: (i, 0)),
        out_shape=hbm((count, length)),
        compiler_params=params(28),
        cost_estimate=cost(6 * count * length * half, 2 * count * length),
        name="forward_rows",
    )(scale, in_hbm(rows), in_hbm(high), in_hbm(low), flip)


def own_rows(place_ref, jump_ref, slab):
    rows = []
    for side in range(2):
        for level in range(slab):
            at = pl.ds(place_ref[0] * slab + level, 1)
            rows.append(jnp.concatenate([jump_ref[g, side, at] for g in range(jump_ref.shape[0])], axis=1))
    return jnp.concatenate(rows, axis=0)


def inverse_kernel(first_call, place_ref, density_ref, even_ref, odd_ref, high_ref, low_ref, flip_ref, *refs):
    half = even_ref.shape[1]

    def joined(even_part, odd_part):
        even = dot3(*split(even_part), high_ref[0], low_ref[0])
        odd = dot3(*split(odd_part), high_ref[1], low_ref[1])
        return even + odd, flipped(*split(even - odd), flip_ref[...])

    out_ref = refs[-3] if first_call else refs[0]
    first, second = joined(even_ref[...], odd_ref[...])
    out_ref[:, :half] = first
    out_ref[:, half:] = second
    if first_call:
        even_jump, odd_jump, below_ref, bottom_ref, _, out_rows_ref, face_ref = refs
        width, slab = face_ref.shape[1], out_rows_ref.shape[0] // 2
        pair = [own_rows(place_ref, jump, slab) for jump in (even_jump, odd_jump)]
        first, second = joined(*pair)
        out_rows_ref[:, 0, :half] = first
        out_rows_ref[:, 0, half:] = second
        liquid, gas = density_ref[0], density_ref[1]
        fractions = below_ref[0] + bottom_ref[0]
        total = fractions * gas + (2.0 - fractions) * liquid
        face_ref[0] = twice_inverse(total) * (out_ref[:width] - out_ref[width:])


def inverse_rows(solved, all_jumps, below, fraction, density, place, width):
    count, length = solved.shape
    half = length // 2
    slab = count // width - 1
    groups, _, depth, lanes = all_jumps.shape
    high, low = halves_of(half_tables(2 * half))
    flip = flip_of(half)
    tables = [fixed(high.shape)] * 2 + [fixed(flip.shape)]
    solved, high, low = in_hbm(solved), in_hbm(high), in_hbm(low)
    smem = pl.BlockSpec(memory_space=pltpu.SMEM)

    def jump(parity):
        return pl.BlockSpec((groups // 2, 2, depth, lanes), lambda i, p: (parity, 0, 0, 0))

    rows = [pl.BlockSpec((2 * width, half), lambda i, p, k=k: (0, k)) for k in range(2)]
    plane = fixed((1, width, 2 * half))
    lower, jump_rows, face = pl.pallas_call(
        functools.partial(inverse_kernel, True),
        grid_spec=pltpu.PrefetchScalarGridSpec(
            num_scalar_prefetch=1,
            grid=(1,),
            in_specs=[smem] + rows + tables + [jump(0), jump(1), plane, plane],
            out_specs=[fixed((2 * width, 2 * half)), fixed((2 * slab, 1, 2 * half)), plane],
        ),
        out_shape=[
            jax.ShapeDtypeStruct((2 * width, 2 * half), F32),
            jax.ShapeDtypeStruct((2 * slab, 1, 2 * half), F32),
            jax.ShapeDtypeStruct((1, width, 2 * half), F32),
        ],
        compiler_params=params(36),
        cost_estimate=cost(28 * width * half * half, 8 * width * half),
        name="inverse_lower",
    )(place, density, solved, solved, high, low, flip, all_jumps, all_jumps, below, fraction)
    rest = (slab - 1) * width
    tile = max(t for t in (width, 2 * width, rest) if rest % t == 0 and t <= 384)
    skip = 2 * width // tile if 2 * width % tile == 0 else None
    if skip is None:
        tile, skip = width, 2
    rows = [pl.BlockSpec((tile, half), lambda i, p, k=k: (skip + i, k)) for k in range(2)]
    upper = pl.pallas_call(
        functools.partial(inverse_kernel, False),
        grid_spec=pltpu.PrefetchScalarGridSpec(
            num_scalar_prefetch=1,
            grid=(rest // tile,),
            in_specs=[smem] + rows + tables,
            out_specs=pl.BlockSpec((tile, 2 * half), lambda i, p: (i, 0)),
        ),
        out_shape=jax.ShapeDtypeStruct((rest, 2 * half), F32),
        compiler_params=params(36),
        cost_estimate=cost(14 * rest * half * half, 4 * rest * half),
        name="inverse_upper",
    )(place, density, solved, solved, high, low, flip)
    return (
        lower.reshape(2, width, 2 * half), upper.reshape(slab - 1, width, 2 * half), jump_rows, face
    )


def ends_kernel(cells, place_ref, field_ref, mixer_ref, ratio_ref, order_ref, out_ref):
    slab, width, lanes = field_ref.shape
    depth = ratio_ref.shape[0]
    ratio = ratio_ref[...]
    step_power = power(ratio, cells)

    def chunk(c, carry):
        right, left, weight = carry
        at = pl.multiple_of(c * cells, cells)
        stacked = field_ref[:, pl.ds(at, cells), :].reshape(slab * cells, lanes)
        high, low = split(stacked)
        modes = dot(mixer_ref[0], jnp.concatenate([high, low, high], axis=0))
        inner = modes[(cells - 1) * depth :]
        for k in reversed(range(cells - 1)):
            inner = inner * ratio + modes[k * depth : (k + 1) * depth]
        for k in range(cells):
            right = right * ratio + modes[k * depth : (k + 1) * depth]
        return right, left + weight * inner, weight * step_power

    zero = jnp.zeros((depth, lanes), F32)
    right, left, _ = lax.fori_loop(0, width // cells, chunk, (zero, zero, zero + 1.0), unroll=2)
    gain = ratio / (1.0 - ratio * ratio)
    left, right = left * gain, right * gain
    per, _, _, part = out_ref.shape
    for g in range(per):
        out_ref[g, 0] = left[:, g * part : (g + 1) * part]
        out_ref[g, 1] = right[:, g * part : (g + 1) * part]


def mode_mixers(depth, groups, cells):
    table = level_table(depth)
    slab = depth // groups
    mixers = []
    for me in range(groups):
        own = table[:, me * slab : (me + 1) * slab]
        mixed = np.einsum("kz,ab->akzb", own, np.eye(cells)).reshape(cells * depth, slab * cells)
        high, low = halves_of(mixed)
        mixers.append(np.concatenate([high, high, low], axis=1))
    return np.stack(mixers)


def end_responses(field, order, place, groups):
    slab, width, length = field.shape
    depth, lanes = slab * groups, length // groups
    cells = divisor_of(width, 8, 16)
    mixers = mode_mixers(depth, groups, cells)
    return pl.pallas_call(
        functools.partial(ends_kernel, cells),
        grid_spec=pltpu.PrefetchScalarGridSpec(
            num_scalar_prefetch=1,
            grid=(groups // 2,),
            in_specs=[
                pl.BlockSpec((slab, width, 2 * lanes), lambda i, p: (0, 0, i)),
                pl.BlockSpec((1,) + mixers.shape[1:], lambda i, p: (p[0], 0, 0)),
                pl.BlockSpec((depth, 2 * lanes), lambda i, p: (0, i)),
                pl.BlockSpec(memory_space=pl.ANY),
            ],
            out_specs=pl.BlockSpec((2, 2, depth, lanes), lambda i, p: (i, 0, 0, 0)),
        ),
        out_shape=jax.ShapeDtypeStruct((groups, 2, depth, lanes), F32),
        compiler_params=params(),
        cost_estimate=cost(2 * mixers[0].size * length * (width // cells), field.size),
        name="end_responses",
    )(place, in_hbm(field), mixers, decay_table(length, depth), order)


def jumps_kernel(width, place_ref, ends_ref, ratio_ref, table_ref, order_ref, order_too_ref, out_ref):
    blocks = ends_ref.shape[0]
    here = place_ref[1]
    ratio = ratio_ref[0]
    block_power = power(ratio, width)
    gain = 1.0 / (1.0 - power(block_power, 2 * blocks))

    def end_of(block, side):
        mirrored = block >= blocks
        source = jnp.where(mirrored, 2 * blocks - 1 - block, block)
        return ends_ref[source, jnp.where(mirrored, 1 - side, side)]

    from_left = jnp.zeros_like(ratio)
    from_right = jnp.zeros_like(ratio)
    for k in range(2 * blocks):
        from_left = from_left * block_power + end_of((here + k) % (2 * blocks), 1)
        from_right = from_right * block_power + end_of((here + 2 * blocks - k) % (2 * blocks), 0)
    from_left = from_left * gain
    from_right = from_right * gain
    jump_left = from_left - (ends_ref[here, 0] + from_right * block_power)
    jump_right = (ends_ref[here, 1] + from_left * block_power) - from_right
    jump_left = jnp.where(place_ref[2] == 1, 0.0, (1.0 - ratio) * jump_left)
    jump_right = jnp.where(place_ref[3] == 1, 0.0, (1.0 - ratio) * jump_right)
    for side, jump in enumerate((jump_left, jump_right)):
        levels = jnp.dot(
            table_ref[...], jump, preferred_element_type=F32, precision=lax.Precision.HIGHEST
        )
        for g in range(out_ref.shape[0]):
            out_ref[g, side] = levels


def jumps(all_ends, orders, place, width, groups):
    _, _, depth, lanes = all_ends.shape
    ratio = decay_table(lanes * groups, depth).reshape(depth, groups, lanes).transpose(1, 0, 2)
    out = (groups, 2, depth, lanes)
    return pl.pallas_call(
        functools.partial(jumps_kernel, width),
        grid_spec=pltpu.PrefetchScalarGridSpec(
            num_scalar_prefetch=1,
            grid=(1,),
            in_specs=[
                fixed(all_ends.shape),
                pl.BlockSpec((1, depth, lanes), lambda i, p: (p[0], 0, 0)),
                fixed((depth, depth)),
                pl.BlockSpec(memory_space=pl.ANY),
                pl.BlockSpec(memory_space=pl.ANY),
            ],
            out_specs=fixed(out),
        ),
        out_shape=jax.ShapeDtypeStruct(out, F32),
        compiler_params=params(),
        cost_estimate=cost(20 * all_ends.size, all_ends.size),
        name="jumps",
    )(place, all_ends, ratio, level_table(depth).T.astype(np.float32), *orders)


def border_kernel(rows, place_ref, jump_ref, nu_ref, mu_ref, ends_ref, order_ref, out_ref, *refs):
    c_ref, prefix_ref, source_ref = refs
    _, _, depth, lanes = jump_ref.shape
    levels, width, _ = out_ref.shape
    first = place_ref[0] * (levels - 1) - 1
    aligned = (width // 2) % rows == 0
    for z in range(depth):
        left, right = jump_ref[0, 0, z : z + 1], jump_ref[0, 1, z : z + 1]
        source_ref[0, z] = jnp.broadcast_to(left - right, (8, lanes))
        source_ref[1, z] = jnp.broadcast_to(left + right, (8, lanes))

    def group(i, carry):
        at = pl.ds(pl.multiple_of(i * rows, rows), rows)
        sigma = nu_ref[at, 0:1] + mu_ref[...]
        if aligned:
            parity = (i * rows) // (width // 2)
        else:
            even = i * rows + lax.broadcasted_iota(jnp.int32, (rows, lanes), 0) < width // 2

        def source(z):
            if aligned:
                return jnp.concatenate([source_ref[parity, z]] * (rows // 8), axis=0)
            pair = [jnp.concatenate([source_ref[k, z]] * (rows // 8), axis=0) for k in range(2)]
            return jnp.where(even, *pair)

        zero = sigma * 0.0
        one = zero + 1.0
        c_ref[0], prefix_ref[0] = zero, zero

        def rise(z, state):
            c, slope, prefix = state
            slope = slope + sigma * c
            return c + slope, slope, prefix + c * source(z)

        def first_level(z, state):
            c, _, prefix = state
            c_ref[0], prefix_ref[0] = c, prefix + c * source(z)
            return rise(z, state)

        state = lax.fori_loop(0, first, rise, (one, zero, zero))
        c, slope, prefix = lax.fori_loop(jnp.maximum(first, 0), first + 1, first_level, state)
        for k in range(1, levels):
            prefix = prefix + c * source(first + k)
            slope = slope + sigma * c
            c_ref[k], prefix_ref[k] = c, prefix
            c = c + slope

        def fall(k, state):
            d, slope, suffix = state
            suffix = suffix + d * source(depth - 1 - k)
            slope = slope + sigma * d
            return d + slope, slope, suffix

        above = depth - first - levels
        d, fall_slope, suffix = lax.fori_loop(0, above, fall, (one, one + one, zero))
        top = levels - 1
        scale = slope * d + c_ref[top] * fall_slope
        inverse = pl.reciprocal(scale, approx=True)
        inverse = inverse * (2.0 - scale * inverse)
        inverse = inverse * (2.0 - scale * inverse)
        inverse = inverse * ends_ref[at, 0:1]
        for k in reversed(range(levels)):
            out_ref[k, at] = inverse * (d * prefix_ref[k] + c_ref[k] * suffix)
            if k:
                suffix = suffix + d * source(first + k)
                fall_slope = fall_slope + sigma * d
                d = d + fall_slope
        return carry

    lax.fori_loop(0, width // rows, group, 0)


def border_solve(all_jumps, order, place, width, length, slab):
    groups, _, depth, lanes = all_jumps.shape
    rows = divisor_of(width, 8, 32)
    modes = spectral_order(width)
    nu = eigenvalues(width)[modes][:, None].astype(np.float32)
    mu = eigenvalues(length)[spectral_order(length)][None, :].astype(np.float32)
    ends = cosine_table(width)[modes][:, :1].astype(np.float32)
    return pl.pallas_call(
        functools.partial(border_kernel, rows),
        grid_spec=pltpu.PrefetchScalarGridSpec(
            num_scalar_prefetch=1,
            grid=(groups,),
            in_specs=[
                pl.BlockSpec((1, 2, depth, lanes), lambda i, p: (i, 0, 0, 0)),
                fixed(nu.shape),
                pl.BlockSpec((1, lanes), lambda i, p: (0, i)),
                fixed(ends.shape),
                pl.BlockSpec(memory_space=pl.ANY),
            ],
            out_specs=pl.BlockSpec((slab + 1, width, lanes), lambda i, p: (0, 0, i)),
            scratch_shapes=[pltpu.VMEM((slab + 1, rows, lanes), F32)] * 2
            + [pltpu.VMEM((2, depth, 8, lanes), F32)],
        ),
        out_shape=jax.ShapeDtypeStruct((slab + 1, width, length), F32),
        compiler_params=params(),
        cost_estimate=cost(20 * depth * width * length, (slab + 1) * width * length),
        name="border_solve",
    )(place, all_jumps, nu, mu, ends, order)


def block_dot(high_ref, low_ref, values):
    high, low = split(values)
    if values.shape[0] % 16 == 0:
        table = jnp.concatenate([high_ref[...], high_ref[...], low_ref[...]], axis=1)
        return dot(table, jnp.concatenate([high, low, high], axis=0))
    return dot(high_ref[...], high) + (dot(high_ref[...], low) + dot(low_ref[...], high))


def eliminate_kernel(place_ref, field_ref, ratio_ref, order_ref, high_ref, low_ref, *refs):
    modes_ref, last_ref, outer_ref, weight_ref = refs
    t, steps = pl.program_id(0), pl.num_programs(0)
    modes = block_dot(high_ref, low_ref, field_ref[0])
    modes_ref[0] = modes
    ratio = ratio_ref[0]

    @pl.when(t == 0)
    def _():
        running = ratio * modes
        last_ref[...], outer_ref[...], weight_ref[...] = running, running, ratio

    @pl.when(t > 0)
    def _():
        running = ratio * (modes + last_ref[...])
        last_ref[...] = running

        @pl.when(t < steps - 1)
        def _():
            outer_ref[...] += weight_ref[...] * running
            weight_ref[...] *= ratio


def eliminate(field, ratios, order, place):
    slab, width, length = field.shape
    lanes = length
    high, low = halves_of(cosine_table(width)[spectral_order(width)])
    plane = fixed((width, lanes))
    return pl.pallas_call(
        eliminate_kernel,
        grid_spec=pltpu.PrefetchScalarGridSpec(
            num_scalar_prefetch=1,
            grid=(slab,),
            in_specs=[
                pl.BlockSpec(
                    (1, width, lanes),
                    lambda t, p: (jnp.where(p[4] == 1, slab - 1 - t, t), 0, 0),
                ),
                pl.BlockSpec((1, width, lanes), lambda t, p: (t, 0, 0)),
                pl.BlockSpec(memory_space=pl.ANY),
                fixed(high.shape),
                fixed(low.shape),
            ],
            out_specs=[pl.BlockSpec((1, width, lanes), lambda t, p: (t, 0, 0)), plane, plane],
            scratch_shapes=[pltpu.VMEM((width, lanes), F32)],
        ),
        out_shape=[hbm((slab, width, lanes)), hbm((width, lanes)), hbm((width, lanes))],
        compiler_params=params(32),
        cost_estimate=cost(6 * width * field.size, 3 * field.size),
        name="eliminate",
    )(place, in_hbm(field), in_hbm(ratios), order, high, low)


def substitute_kernel(place_ref, modes_ref, ratio_ref, prev_ratio_ref, in_ref, next_ref, back_ref, border_ref, order_ref, high_ref, low_ref, out_ref, kept):
    slab = modes_ref.shape[0]
    upper = place_ref[4] == 1
    running = in_ref[...]
    for t in range(slab):
        running = ratio_ref[t] * (modes_ref[t] + running)
        kept[t] = running

    def emit(t, values):
        level = jnp.where(upper, slab - t, t + 1)
        out_ref[level] = block_dot(high_ref, low_ref, values + border_ref[level])

    beyond = next_ref[...] + back_ref[...]
    following = beyond
    for t in reversed(range(slab)):
        following = kept[t] + ratio_ref[t] * following
        emit(t, following)
    outside = in_ref[...] + prev_ratio_ref[0] * following
    values = jnp.where(upper, beyond, outside) + border_ref[0]
    out_ref[0] = block_dot(high_ref, low_ref, values)


def substitute(modes, ratios, incoming, following, back, border, order, place):
    slab, width, size = modes.shape
    lanes = divisor_of(size, 128, 384)
    per = size // lanes
    high, low = halves_of(cosine_table(width)[spectral_order(width)].T)
    plane = pl.BlockSpec((width, lanes), lambda i, p: (0, i))
    return pl.pallas_call(
        substitute_kernel,
        grid_spec=pltpu.PrefetchScalarGridSpec(
            num_scalar_prefetch=1,
            grid=(per,),
            in_specs=[
                pl.BlockSpec((slab, width, lanes), lambda i, p: (0, 0, i)),
                pl.BlockSpec((slab, width, lanes), lambda i, p: (0, 0, i)),
                pl.BlockSpec((1, width, lanes), lambda i, p: (slab, 0, i)),
                plane,
                plane,
                plane,
                pl.BlockSpec((slab + 1, width, lanes), lambda i, p: (0, 0, i)),
                pl.BlockSpec(memory_space=pl.ANY),
                fixed(high.shape),
                fixed(low.shape),
            ],
            out_specs=pl.BlockSpec((slab + 1, width, lanes), lambda i, p: (0, 0, i)),
            scratch_shapes=[pltpu.VMEM((slab, width, lanes), F32)],
        ),
        out_shape=hbm((slab + 1, width, size)),
        compiler_params=params(),
        cost_estimate=cost(9 * width * modes.size, 4 * modes.size),
        name="substitute",
    )(
        place, in_hbm(modes), in_hbm(ratios), in_hbm(ratios), incoming, following, back, border,
        order, high, low,
    )


def relay_kernel(last_ref, through_ref, in_ref, order_ref, out_ref):
    through = through_ref[0]
    for t in range(1, through_ref.shape[0]):
        through = through * through_ref[t]
    out_ref[...] = last_ref[...] + through * in_ref[...]


def row_tile(width):
    return divisor_of(width, 8, 48)


def relay(last, ratios, slab, incoming, order, chunk):
    width, lanes = last.shape
    tile = row_tile(width)
    own = pl.BlockSpec((tile, lanes), lambda i: (i, 0))
    return pl.pallas_call(
        relay_kernel,
        grid=(width // tile,),
        in_specs=[
            own,
            pl.BlockSpec((slab, tile, lanes), lambda i: (0, i, chunk)),
            own,
            pl.BlockSpec(memory_space=pl.ANY),
        ],
        out_specs=own,
        out_shape=jax.ShapeDtypeStruct(last.shape, F32),
        compiler_params=params(),
        cost_estimate=cost(2 * last.size, 4 * last.size),
        name="relay",
    )(in_hbm(last), in_hbm(ratios), incoming, order)


def turn_kernel(slab, place_ref, mine_ref, theirs_ref, in_ref, outer_ref, next_ref, ratios_ref, *refs):
    message_ref, follow_ref = refs[-2:]
    innermost = place_ref[5] == 1

    mine, theirs, follow = mine_ref[...], theirs_ref[...], next_ref[...]
    through = ratios_ref[0]
    weight, outer_in = through, through
    for t in range(1, slab):
        ratio = ratios_ref[t]
        through = through * ratio
        if t < slab - 1:
            outer_in = outer_in + weight * through
            weight = weight * ratio
    other = ratios_ref[slab + 1]
    meet = inverted(1.0 - ratio * other)
    inner = jnp.where(innermost, (mine + ratio * theirs) * meet, mine + ratio * follow)
    follow_ref[...] = jnp.where(innermost, (theirs + other * mine) * meet, follow)
    message_ref[...] = outer_ref[...] + outer_in * in_ref[...] + weight * inner


def turn(mine, theirs, incoming, outer, following, ratios, orders, place, chunk):
    width, lanes = mine.shape
    tile = row_tile(width)
    own = pl.BlockSpec((tile, lanes), lambda i, p: (i, 0))
    planes = ratios.shape[0]
    return pl.pallas_call(
        functools.partial(turn_kernel, planes - 2),
        grid_spec=pltpu.PrefetchScalarGridSpec(
            num_scalar_prefetch=1,
            grid=(width // tile,),
            in_specs=[own] * 5
            + [
                pl.BlockSpec((planes, tile, lanes), lambda i, p: (0, i, chunk)),
            ]
            + [pl.BlockSpec(memory_space=pl.ANY)] * len(orders),
            out_specs=[own] * 2,
        ),
        out_shape=[jax.ShapeDtypeStruct(mine.shape, F32), hbm(mine.shape)],
        compiler_params=params(),
        cost_estimate=cost(12 * mine.size, 12 * mine.size),
        name="turn",
    )(place, mine, theirs, incoming, in_hbm(outer), following, in_hbm(ratios), *orders)


def inverted(value):
    guess = pl.reciprocal(value, approx=True)
    guess = guess * (2.0 - value * guess)
    return guess * (2.0 - value * guess)


def sequence(sigma, upper, steps):
    zero = sigma * 0.0
    slope = zero + jnp.where(upper, 2.0, 0.0).astype(F32)

    def advance(_, state):
        value, slope = state
        slope = slope + sigma * value
        return value + slope, slope

    return lax.fori_loop(0, steps, advance, (zero + 1.0, slope))


def ratio_kernel(steps, lanes, place_ref, nu_ref, mu_ref, ratios_ref):
    planes, rows, length = ratios_ref.shape
    slab = planes - 2
    upper, rank = place_ref[4] == 1, place_ref[8]

    def group(i, carry):
        at = pl.ds(pl.multiple_of(i * lanes, lanes), lanes)
        sigma = nu_ref[...] + mu_ref[:, at]
        value, slope = sequence(sigma, upper, rank * slab)
        ratios_ref[slab, :, at] = jnp.where(rank == 0, 0.0, (value - slope) * inverted(value))
        for t in range(slab):
            slope = slope + sigma * value
            following = value + slope
            ratios_ref[t, :, at] = value * inverted(following)
            value = following
        value, slope = sequence(sigma, jnp.logical_not(upper), steps)
        ratios_ref[slab + 1, :, at] = (value - slope) * inverted(value)
        return carry

    lax.fori_loop(0, length // lanes, group, 0)


def pivots(width, length, slab, groups, place):
    rows = divisor_of(width, 8, 32)
    lanes = divisor_of(length, 128, 512)
    nu = eigenvalues(width)[spectral_order(width)][:, None].astype(np.float32)
    mu = eigenvalues(length)[spectral_order(length)][None, :].astype(np.float32)
    return pl.pallas_call(
        functools.partial(ratio_kernel, groups // 2 * slab, lanes),
        grid_spec=pltpu.PrefetchScalarGridSpec(
            num_scalar_prefetch=1,
            grid=(width // rows,),
            in_specs=[pl.BlockSpec((rows, 1), lambda i, p: (i, 0)), fixed(mu.shape)],
            out_specs=pl.BlockSpec((slab + 2, rows, length), lambda i, p: (0, i, 0)),
        ),
        out_shape=hbm((slab + 2, width, length)),
        compiler_params=params(),
        cost_estimate=cost(120 * width * length, 6 * width * length),
        name="ratios",
    )(place, nu, mu)


def cut_kernel(d_top, f_top, d_first, f_first, d_last, f_last, top_ref, fraction_ref, first_ref, last_ref):
    slab = d_first.shape[0]
    top_ref[...] = d_top[...]
    fraction_ref[...] = f_top[...]
    first_ref[:slab] = d_first[:, 0:1]
    first_ref[slab:] = f_first[:, 0:1]
    last_ref[:slab] = d_last[:, 7:8]
    last_ref[slab:] = f_last[:, 7:8]


def cut_borders(direction, fraction):
    slab, width, lanes = direction.shape
    top = pl.BlockSpec((1, width, lanes), lambda i: (slab - 1, 0, 0))
    first = pl.BlockSpec((slab, 8, lanes), lambda i: (0, 0, 0))
    last = pl.BlockSpec((slab, 8, lanes), lambda i: (0, width // 8 - 1, 0))
    shapes = [(1, width, lanes)] * 2 + [(2 * slab, 1, lanes)] * 2
    direction, fraction = in_hbm(direction), in_hbm(fraction)
    return pl.pallas_call(
        cut_kernel,
        grid=(1,),
        in_specs=[top, top, first, first, last, last],
        out_specs=[fixed(shape) for shape in shapes],
        out_shape=[jax.ShapeDtypeStruct(shape, F32) for shape in shapes],
        compiler_params=params(),
        cost_estimate=cost(0, 4 * width * lanes),
        name="cut_borders",
    )(direction, fraction, direction, fraction, direction, fraction)


def neighbours(length):
    up = [(i, i + 1) for i in range(length - 1)]
    return up, [(j, i) for i, j in up]


def twice_inverse(total):
    guess = pl.reciprocal(total, approx=True)
    guess = guess * (2.0 - total * guess)
    return guess + guess


def operator_kernel(n_dots, n_kept, with_levels, place_ref, density_ref, *refs):
    if with_levels:
        (f_low, f_low_prev, f_low_next, f_ref, f_prev, f_next), refs = refs[:6], refs[6:]
    else:
        (f_ref, f_prev, f_next, f_below, f_below_too), refs = refs[:5], refs[5:]
    (f_lo, f_hi, d_ref, d_prev, d_next, d_below, d_lo, d_hi), refs = refs[:8], refs[8:]
    dot_refs = refs[:n_dots]
    face_ref, kept_ref, _, image_ref, out_sums_ref, out_face_ref = refs[n_dots : 6 + n_dots]
    field, dense, before_ref, sums_ref = refs[6 + n_dots :]
    slab, tile, lanes = image_ref.shape
    step, steps = pl.program_id(0), pl.num_programs(0)
    at_left = jnp.logical_and(place_ref[2] == 1, step == 0)
    at_right = jnp.logical_and(place_ref[3] == 1, step == steps - 1)
    at_bottom, at_top = place_ref[6] == 1, place_ref[7] == 1
    liquid, gas = density_ref[0], density_ref[1]

    def mixed(fraction):
        return fraction * gas + (1.0 - fraction) * liquid

    own = slice(8, 8 + tile)
    if with_levels:
        field[0:2, own] = f_low[...]
        field[2:, own] = f_ref[...]
    else:
        field[0:1, own] = f_below[...] + f_below_too[...]
        field[1:, own] = f_ref[...]
    dense[1:, own] = mixed(d_ref[...])
    dense[0:1, own] = mixed(d_below[...])

    @pl.when(step == 0)
    def _():
        field[1:, 7:8] = field[1:, 8:9] + f_lo[...] if with_levels else f_lo[...]
        dense[1:, 7:8] = mixed(d_lo[...])
        sums_ref[...] = jnp.zeros_like(sums_ref)

    @pl.when(step > 0)
    def _():
        if with_levels:
            field[1:2, 7:8] = f_low_prev[1:2, 7:8]
            field[2:, 7:8] = f_prev[:, 7:8]
        else:
            field[1:, 7:8] = f_prev[:, 7:8]
        dense[1:, 7:8] = mixed(d_prev[:, 7:8])

    @pl.when(step == steps - 1)
    def _():
        last_row = field[1:, 7 + tile : 8 + tile]
        field[1:, 8 + tile : 9 + tile] = last_row - f_hi[...] if with_levels else f_hi[...]
        dense[1:, 8 + tile : 9 + tile] = mixed(d_hi[...])

    @pl.when(step < steps - 1)
    def _():
        if with_levels:
            field[1:2, 8 + tile : 9 + tile] = f_low_next[1:2, 0:1]
            field[2:, 8 + tile : 9 + tile] = f_next[:, 0:1]
        else:
            field[1:, 8 + tile : 9 + tile] = f_next[:, 0:1]
        dense[1:, 8 + tile : 9 + tile] = mixed(d_next[:, 0:1])

    lane_ids = lax.broadcasted_iota(jnp.int32, (8, lanes), 1)
    row_ids = lax.broadcasted_iota(jnp.int32, (8, lanes), 0)
    has_right = (lane_ids < lanes - 1).astype(F32)

    def face(mid, rho, neighbour, rho_next):
        return twice_inverse(rho + rho_next) * (mid - neighbour)

    def next_row(ref, z, at, mid):
        following = ref[z, pl.ds(at + 8, 8)]
        return jnp.where(row_ids == 7, pltpu.roll(following, 7, 0), pltpu.roll(mid, 7, 0))

    def face_after(z, at, mid, rho):
        return face(mid, rho, next_row(field, z, at, mid), next_row(dense, z, at, rho))

    for level in range(slab):
        first = face_after(level + 1, 0, field[level + 1, 0:8], dense[level + 1, 0:8])
        before_ref[level] = jnp.where(at_left, 0.0, pltpu.roll(first, 1, 0))

    def rows(i, carry):
        at = pl.multiple_of(8 + 8 * i, 8)
        own = pl.ds(pl.multiple_of(8 * i, 8), 8)
        at_end = jnp.logical_and(at_right, i == tile // 8 - 1)
        mid, rho = field[0, pl.ds(at, 8)], dense[0, pl.ds(at, 8)]
        up, rho_up = field[1, pl.ds(at, 8)], dense[1, pl.ds(at, 8)]
        above = jnp.where(at_bottom, 0.0, face(mid, rho, up, rho_up))
        out_face_ref[0, own] = above
        totals = [mid * above] + [jnp.zeros((8, lanes), F32)] * n_dots
        if n_dots > 1:
            totals[-1] = jnp.where(at_bottom, 0.0, mid * face_ref[0, own])
        for level in range(slab):
            below = above
            mid, rho = up, rho_up
            if level < slab - 1:
                up, rho_up = field[level + 2, pl.ds(at, 8)], dense[level + 2, pl.ds(at, 8)]
                above = face(mid, rho, up, rho_up)
            else:
                above = jnp.where(at_top, twice_inverse(rho) * mid, 0.0)
            after = face_after(level + 1, at, mid, rho)
            after = jnp.where(jnp.logical_and(at_end, row_ids == 7), 0.0, after)
            shifted = pltpu.roll(after, 1, 0)
            before = jnp.where(row_ids == 0, before_ref[level], shifted)
            before_ref[level] = shifted
            right = has_right * face(
                mid, rho, pltpu.roll(mid, lanes - 1, 1), pltpu.roll(rho, lanes - 1, 1)
            )
            image = (above - below) + (after - before) + (right - pltpu.roll(right, 1, 1))
            image_ref[level, own] = image
            totals[0] = totals[0] + mid * image
            for k in range(n_dots):
                totals[k + 1] = totals[k + 1] + mid * dot_refs[k][level, own]
        for k in range(n_dots + 1):
            sums_ref[k] += totals[k]
        return carry

    lax.fori_loop(0, tile // 8, rows, 0)

    @pl.when(step == steps - 1)
    def _():
        group_ids = lax.broadcasted_iota(jnp.int32, (1, 128), 1) // 16
        packed = jnp.where(group_ids < n_kept, kept_ref[0], 0.0)
        for k in range(n_dots + 1):
            line = jnp.sum(sums_ref[k], axis=0, keepdims=True)
            line = sum(line[:, j : j + 128] for j in range(0, lanes, 128))
            for shift in (64, 32, 16):
                line = line + pltpu.roll(line, shift, 1)
            packed = jnp.where(group_ids == n_kept + k, line, packed)
        for k in range(out_sums_ref.shape[0]):
            out_sums_ref[k] = packed


def apply_operator(fields, belows, sides, fraction, border, density, others, face, kept, n_kept, copies, order, place, name):
    slab, width, lanes = fraction.shape
    with_levels = len(fields) > 1
    tile = divisor_of(width, 8, 48)
    per = tile // 8
    last = width // 8 - 1

    def triple(levels):
        return [
            pl.BlockSpec((levels, tile, lanes), lambda i, p: (0, i, 0)),
            pl.BlockSpec((levels, 8, lanes), lambda i, p: (0, jnp.maximum(i * per - 1, 0), 0)),
            pl.BlockSpec((levels, 8, lanes), lambda i, p: (0, jnp.minimum((i + 1) * per, last), 0)),
        ]

    plane = pl.BlockSpec((1, tile, lanes), lambda i, p: (0, i, 0))

    def borders(planes, *places):
        return [plane] * planes + [
            pl.BlockSpec((slab, 1, lanes), lambda i, p, k=k: (k, 0, 0)) for k in places
        ]

    own = pl.BlockSpec((slab, tile, lanes), lambda i, p: (0, i, 0))
    specs = [pl.BlockSpec(memory_space=pltpu.SMEM)]
    for field in fields:
        specs += triple(field.shape[0])
    specs += borders(0, 0, 1) if with_levels else borders(2, 0, 0)
    specs += triple(slab) + borders(1, 1, 1)
    specs += [own] * len(others)
    specs += [plane, fixed((1, 1, 128)), pl.BlockSpec(memory_space=pl.ANY)]
    planes = slab * (3 + len(others)) + 1
    operands = [field for field in fields for _ in range(3)] + ([] if with_levels else list(belows))
    return pl.pallas_call(
        functools.partial(operator_kernel, len(others), n_kept, with_levels),
        grid_spec=pltpu.PrefetchScalarGridSpec(
            num_scalar_prefetch=1,
            grid=(width // tile,),
            in_specs=specs,
            out_specs=[own, fixed((copies, 1, 128)), plane],
            scratch_shapes=[pltpu.VMEM((slab + 1, tile + 16, lanes), F32)] * 2
            + [
                pltpu.VMEM((slab, 8, lanes), F32),
                pltpu.VMEM((len(others) + 1, 8, lanes), F32),
            ],
        ),
        out_shape=[
            jax.ShapeDtypeStruct((slab, width, lanes), F32) if with_levels else hbm((slab, width, lanes)),
            jax.ShapeDtypeStruct((copies, 1, 128), F32),
            hbm((1, width, lanes)),
        ],
        compiler_params=params(28),
        cost_estimate=cost(100 * slab * width * lanes, planes * width * lanes),
        name=name,
    )(
        place, density, *operands, *sides,
        fraction, fraction, fraction, *border, *others, face, kept, order,
    )


def update_kernel(sums_ref, low_ref, high_ref, direction_ref, solution_ref, residual_ref, old_ref, new_ref, old_face_ref, new_face_ref, *refs):
    solution_out, residual_out, direction_out = refs
    slab, _, lanes = direction_ref.shape
    packed = jnp.sum(sums_ref[...], axis=0)
    group_ids = lax.broadcasted_iota(jnp.int32, (1, 128), 1) // 16
    t0, t3, t4, t2, t1 = (
        jnp.broadcast_to(
            jnp.sum(jnp.where(group_ids == k, packed, 0.0), axis=1, keepdims=True), (1, 128)
        )
        for k in range(5)
    )
    t5 = t1
    conjugate = -t1 / t0
    along_r = t2 + conjugate * t3
    curvature = t4 + conjugate * (t1 + t5) + conjugate * conjugate * t0
    step_len = along_r / curvature
    conjugate = jnp.concatenate([conjugate] * (lanes // 128), axis=1)
    step_len = jnp.concatenate([step_len] * (lanes // 128), axis=1)
    for level in range(slab):
        precond = high_ref[level - 1] if level else low_ref[0]
        turned = precond + conjugate * direction_ref[level]
        direction_out[level] = turned
        solution_out[level] = solution_ref[level] + step_len * turned
        image = new_ref[level] + conjugate * old_ref[level]
        if level == slab - 1:
            image = image + (new_face_ref[0] + conjugate * old_face_ref[0])
        residual_out[level] = residual_ref[level] - step_len * image


def update(sums, precond_low, precond_high, direction, solution, residual, image_old, image_new, old_face, new_face):
    slab, width, lanes = direction.shape
    tile = divisor_of(width, 8, 24)
    own = pl.BlockSpec((slab, tile, lanes), lambda i: (0, i, 0))
    return pl.pallas_call(
        update_kernel,
        grid=(width // tile,),
        in_specs=[
            fixed(sums.shape),
            pl.BlockSpec((1, tile, lanes), lambda i: (1, i, 0)),
            pl.BlockSpec((slab - 1, tile, lanes), lambda i: (0, i, 0)),
        ]
        + [own] * 5
        + [pl.BlockSpec((1, tile, lanes), lambda i: (0, i, 0))] * 2,
        out_specs=[own] * 3,
        out_shape=[jax.ShapeDtypeStruct(direction.shape, F32)] * 3,
        compiler_params=params(28),
        cost_estimate=cost(10 * direction.size, 10 * direction.size),
        name="update",
    )(
        sums, precond_low, precond_high, in_hbm(direction), in_hbm(solution), in_hbm(residual),
        in_hbm(image_old), image_new, old_face, new_face,
    )


def body(solution, residual, direction, volume_fraction, density):
    slab, width, length = residual.shape
    groups, plane_parts = lax.axis_size("gz"), lax.axis_size("xy")
    half = groups // 2
    me, here = lax.axis_index("gz"), lax.axis_index("xy")
    upper = me >= half
    rank = jnp.where(upper, groups - 1 - me, me)
    innermost = rank == half - 1
    flags = [me, here, here == 0, here == plane_parts - 1, upper, innermost, me == 0, me == groups - 1]
    place = jnp.stack(flags + [rank]).astype(jnp.int32)
    scale = (2.0 / (1.0 / density[0] + 1.0 / density[1])).reshape(1)

    up, down = neighbours(groups)
    left, right = neighbours(plane_parts)[::-1]
    top, fraction_top, first_rows, last_rows = cut_borders(direction, volume_fraction)
    fraction_below = lax.ppermute(fraction_top, "gz", up)
    below = lax.ppermute(top, "gz", up[1:]) if up[1:] else jnp.zeros_like(top)
    sides = (lax.ppermute(last_rows, "xy", right), lax.ppermute(first_rows, "xy", left))

    spectral = forward_rows(residual.reshape(slab * width, length), scale)
    spectral = spectral.reshape(slab, width, length)
    ratios = pivots(width, length, slab, groups, place)
    inward = [[(s - 1, s), (groups - s, groups - 1 - s)] for s in range(1, half)]
    outward = [[(j, i) for i, j in pairs] for pairs in reversed(inward)]
    across = [(half - 1, half), (half, half - 1)]
    modes, last, outer = eliminate(spectral, ratios, fraction_below, place)
    zero = jnp.zeros_like(last)
    parts = end_responses(spectral, last, place, groups)
    late_top, parts = lax.optimization_barrier((top, parts))
    below_too = lax.ppermute(late_top, "gz", up[:1])
    ends = jnp.sum(lax.all_to_all(parts, "gz", 0, 0, tiled=True), axis=0)
    incoming, mine = zero, last
    for k, pairs in enumerate(inward):
        arrived = lax.ppermute(mine, "gz", pairs)
        incoming = incoming + arrived if k else arrived
        mine = relay(last, ratios, slab, incoming, below, 0)
    ends, mine = lax.optimization_barrier((ends, mine))
    all_ends = lax.all_to_all(
        jnp.broadcast_to(ends[None], (plane_parts,) + ends.shape), "xy", 0, 0, tiled=True
    )
    all_jumps = lax.all_to_all(jumps(all_ends, sides, place, width, groups), "gz", 0, 0, tiled=True)
    theirs = lax.ppermute(mine, "gz", across)
    orders = (below_too, all_jumps)
    message, following = turn(mine, theirs, incoming, outer, zero, ratios, orders, place, 0)
    back = zero
    for k, pairs in enumerate(outward):
        if k:
            message, following = turn(
                mine, theirs, incoming, outer, following + back, ratios, orders, place, 0
            )
        back = lax.ppermute(message, "gz", pairs)

    belows = (below, below_too)
    border = (fraction_below,) + sides
    nothing = jnp.zeros((1, 1, 128), F32)
    image_old, sums_old, old_face = apply_operator(
        [in_hbm(direction)], belows, sides, in_hbm(volume_fraction), border, density,
        [in_hbm(residual)], below, nothing, 0, 1, message, place, "image_old"
    )
    old_above = lax.ppermute(old_face, "gz", down)
    jumped = border_solve(all_jumps, message, place, width, length, slab)
    solved = substitute(modes, ratios, incoming, following, back, jumped, sums_old, place)
    precond_low, precond_high, jump_rows, new_face = inverse_rows(
        solved.reshape((slab + 1) * width, length), all_jumps, fraction_below,
        in_hbm(volume_fraction), density, place, width
    )
    new_above = lax.ppermute(new_face, "gz", down)
    image_new, sums, _ = apply_operator(
        [precond_low, precond_high], belows, (jump_rows, jump_rows),
        in_hbm(volume_fraction), border, density, [in_hbm(residual), in_hbm(image_old)],
        in_hbm(old_face), sums_old, 2, groups * plane_parts, sums_old, place, "image_new"
    )
    gathered = lax.all_to_all(sums, ("gz", "xy"), 0, 0, tiled=True)
    new_solution, new_residual, new_direction = update(
        gathered, precond_low, precond_high, direction, solution, residual, image_old, image_new,
        old_above, new_above
    )
    return (new_solution, new_residual, new_direction)


def solution(mesh):
    placed = P("gz", "xy", None)
    return jax.shard_map(
        body,
        mesh=mesh,
        in_specs=(placed, placed, placed, placed, P()),
        out_specs=(placed, placed, placed),
        check_vma=False,
    )
```

```python
import functools

import jax
import jax.numpy as jnp
import numpy as np
from jax import lax
from jax.experimental import pallas as pl
from jax.experimental.pallas import tpu as pltpu
from jax.sharding import PartitionSpec as P

F32 = jnp.float32
BF16 = jnp.bfloat16
MIB = 1024 * 1024


def divisor_of(length, unit, largest):
    return max(t for t in range(unit, largest + 1, unit) if length % t == 0)


def halves_of(table):
    high = table.astype(BF16)
    low = (table - high.astype(np.float64)).astype(BF16)
    return high, low


def split(values):
    high = values.astype(BF16)
    return high, (values - high.astype(F32)).astype(BF16)


def dot(a, b):
    return jnp.dot(a, b, preferred_element_type=F32)


def dot3(a_high, a_low, b_high, b_low):
    return dot(a_high, b_high) + (dot(a_low, b_high) + dot(a_high, b_low))


def cosine_table(length):
    freq = np.arange(length)[:, None]
    cell = np.arange(length)[None, :]
    angles = np.pi / (2 * length) * (freq * (2 * cell + 1) % (4 * length))
    return np.where(freq == 0, np.sqrt(1.0 / length), np.sqrt(2.0 / length)) * np.cos(angles)


def spectral_order(length):
    return np.concatenate([np.arange(0, length, 2), np.arange(1, length, 2)])


def half_tables(length):
    half = length // 2
    return cosine_table(length)[spectral_order(length), :half].reshape(2, half, half)


def eigenvalues(length):
    return 4.0 * np.sin(np.pi * np.arange(length) / (2 * length)) ** 2


def level_table(depth):
    modes = np.arange(depth)[:, None]
    levels = np.arange(depth)[None, :]
    return np.sqrt(2.0 / depth) * np.cos(np.pi * (2 * modes + 1) * (2 * levels + 1) / (4 * depth))


def decay_table(length, depth):
    mu = eigenvalues(length)[spectral_order(length)]
    lam = 4.0 * np.sin(np.pi * (2 * np.arange(depth) + 1) / (4 * depth)) ** 2
    excess = lam[:, None] + mu[None, :]
    return (1.0 + excess / 2 - np.sqrt(excess + excess * excess / 4)).astype(np.float32)


def flip_matrix(size):
    return np.eye(size)[::-1].astype(BF16)


def flipped(high, low, flip):
    size = flip.shape[0]
    count = high.shape[1] // size
    blocks = []
    for i in range(count):
        part = slice((count - 1 - i) * size, (count - i) * size)
        blocks.append(dot(high[:, part], flip) + dot(low[:, part], flip))
    return jnp.concatenate(blocks, axis=1)


def power(base, exponent):
    result = None
    while exponent:
        if exponent & 1:
            result = base if result is None else result * base
        base = base * base
        exponent >>= 1
    return result


def fixed(shape):
    return pl.BlockSpec(shape, lambda *_: (0,) * len(shape))


def in_hbm(array):
    return pltpu.with_memory_space_constraint(array, pltpu.HBM)


def hbm(shape):
    return pltpu.HBM(shape, F32)


def params(mib=24):
    return pltpu.CompilerParams(vmem_limit_bytes=mib * MIB)


def cost(flops, count):
    return pl.CostEstimate(flops=int(flops) // 16, bytes_accessed=int(count) // 4, transcendentals=0)


def forward_kernel(scale_ref, rows_ref, high_ref, low_ref, flip_ref, out_ref):
    half = rows_ref.shape[1] // 2
    first, second = rows_ref[:, :half], rows_ref[:, half:]
    mirror = flipped(*split(second), flip_ref[...])
    scale = scale_ref[0]
    for parity, folded in enumerate((first + mirror, first - mirror)):
        out = dot3(*split(folded), high_ref[parity], low_ref[parity])
        out_ref[:, parity * half : (parity + 1) * half] = scale * out


def flip_of(half):
    return flip_matrix(256 if half % 256 == 0 else 128)


def forward_rows(rows, scale):
    count, length = rows.shape
    half = length // 2
    tile = divisor_of(count, 8, 256)
    high, low = halves_of(half_tables(length).transpose(0, 2, 1))
    flip = flip_of(half)
    return pl.pallas_call(
        forward_kernel,
        grid=(count // tile,),
        in_specs=[
            pl.BlockSpec(memory_space=pltpu.SMEM),
            pl.BlockSpec((tile, length), lambda i: (i, 0)),
            fixed(high.shape),
            fixed(low.shape),
            fixed(flip.shape),
        ],
        out_specs=pl.BlockSpec((tile, length), lambda i: (i, 0)),
        out_shape=hbm((count, length)),
        compiler_params=params(28),
        cost_estimate=cost(6 * count * length * half, 2 * count * length),
        name="forward_rows",
    )(scale, in_hbm(rows), in_hbm(high), in_hbm(low), flip)


def own_rows(place_ref, jump_ref, slab):
    rows = []
    for side in range(2):
        for level in range(slab):
            at = pl.ds(place_ref[0] * slab + level, 1)
            rows.append(jnp.concatenate([jump_ref[g, side, at] for g in range(jump_ref.shape[0])], axis=1))
    return jnp.concatenate(rows, axis=0)


def inverse_kernel(first_call, place_ref, density_ref, even_ref, odd_ref, high_ref, low_ref, flip_ref, *refs):
    half = even_ref.shape[1]

    def joined(even_part, odd_part):
        even = dot3(*split(even_part), high_ref[0], low_ref[0])
        odd = dot3(*split(odd_part), high_ref[1], low_ref[1])
        return even + odd, flipped(*split(even - odd), flip_ref[...])

    out_ref = refs[-3] if first_call else refs[0]
    first, second = joined(even_ref[...], odd_ref[...])
    out_ref[:, :half] = first
    out_ref[:, half:] = second
    if first_call:
        even_jump, odd_jump, below_ref, bottom_ref, _, out_rows_ref, face_ref = refs
        width, slab = face_ref.shape[1], out_rows_ref.shape[0] // 2
        pair = [own_rows(place_ref, jump, slab) for jump in (even_jump, odd_jump)]
        first, second = joined(*pair)
        out_rows_ref[:, 0, :half] = first
        out_rows_ref[:, 0, half:] = second
        liquid, gas = density_ref[0], density_ref[1]
        fractions = below_ref[0] + bottom_ref[0]
        total = fractions * gas + (2.0 - fractions) * liquid
        face_ref[0] = twice_inverse(total) * (out_ref[:width] - out_ref[width:])


def inverse_rows(solved, all_jumps, below, fraction, density, place, width):
    count, length = solved.shape
    half = length // 2
    slab = count // width - 1
    groups, _, depth, lanes = all_jumps.shape
    high, low = halves_of(half_tables(2 * half))
    flip = flip_of(half)
    tables = [fixed(high.shape)] * 2 + [fixed(flip.shape)]
    solved, high, low = in_hbm(solved), in_hbm(high), in_hbm(low)
    smem = pl.BlockSpec(memory_space=pltpu.SMEM)

    def jump(parity):
        return pl.BlockSpec((groups // 2, 2, depth, lanes), lambda i, p: (parity, 0, 0, 0))

    rows = [pl.BlockSpec((2 * width, half), lambda i, p, k=k: (0, k)) for k in range(2)]
    plane = fixed((1, width, 2 * half))
    lower, jump_rows, face = pl.pallas_call(
        functools.partial(inverse_kernel, True),
        grid_spec=pltpu.PrefetchScalarGridSpec(
            num_scalar_prefetch=1,
            grid=(1,),
            in_specs=[smem] + rows + tables + [jump(0), jump(1), plane, plane],
            out_specs=[fixed((2 * width, 2 * half)), fixed((2 * slab, 1, 2 * half)), plane],
        ),
        out_shape=[
            hbm((2 * width, 2 * half)),
            jax.ShapeDtypeStruct((2 * slab, 1, 2 * half), F32),
            jax.ShapeDtypeStruct((1, width, 2 * half), F32),
        ],
        compiler_params=params(36),
        cost_estimate=cost(28 * width * half * half, 8 * width * half),
        name="inverse_lower",
    )(place, density, solved, solved, high, low, flip, all_jumps, all_jumps, below, fraction)
    rest = (slab - 1) * width
    tile = max(t for t in (width, 2 * width, rest) if rest % t == 0 and t <= 384)
    skip = 2 * width // tile if 2 * width % tile == 0 else None
    if skip is None:
        tile, skip = width, 2
    rows = [pl.BlockSpec((tile, half), lambda i, p, k=k: (skip + i, k)) for k in range(2)]
    upper = pl.pallas_call(
        functools.partial(inverse_kernel, False),
        grid_spec=pltpu.PrefetchScalarGridSpec(
            num_scalar_prefetch=1,
            grid=(rest // tile,),
            in_specs=[smem] + rows + tables,
            out_specs=pl.BlockSpec((tile, 2 * half), lambda i, p: (i, 0)),
        ),
        out_shape=hbm((rest, 2 * half)),
        compiler_params=params(36),
        cost_estimate=cost(14 * rest * half * half, 4 * rest * half),
        name="inverse_upper",
    )(place, density, solved, solved, high, low, flip)
    return (
        lower.reshape(2, width, 2 * half), upper.reshape(slab - 1, width, 2 * half), jump_rows, face
    )


def ends_kernel(cells, place_ref, field_ref, mixer_ref, ratio_ref, order_ref, out_ref):
    slab, width, lanes = field_ref.shape
    depth = ratio_ref.shape[0]
    ratio = ratio_ref[...]
    step_power = power(ratio, cells)

    def chunk(c, carry):
        right, left, weight = carry
        at = pl.multiple_of(c * cells, cells)
        stacked = field_ref[:, pl.ds(at, cells), :].reshape(slab * cells, lanes)
        high, low = split(stacked)
        modes = dot(mixer_ref[0], jnp.concatenate([high, low, high], axis=0))
        inner = modes[(cells - 1) * depth :]
        for k in reversed(range(cells - 1)):
            inner = inner * ratio + modes[k * depth : (k + 1) * depth]
        for k in range(cells):
            right = right * ratio + modes[k * depth : (k + 1) * depth]
        return right, left + weight * inner, weight * step_power

    zero = jnp.zeros((depth, lanes), F32)
    right, left, _ = lax.fori_loop(0, width // cells, chunk, (zero, zero, zero + 1.0), unroll=2)
    gain = ratio / (1.0 - ratio * ratio)
    left, right = left * gain, right * gain
    per, _, _, part = out_ref.shape
    for g in range(per):
        out_ref[g, 0] = left[:, g * part : (g + 1) * part]
        out_ref[g, 1] = right[:, g * part : (g + 1) * part]


def mode_mixers(depth, groups, cells):
    table = level_table(depth)
    slab = depth // groups
    mixers = []
    for me in range(groups):
        own = table[:, me * slab : (me + 1) * slab]
        mixed = np.einsum("kz,ab->akzb", own, np.eye(cells)).reshape(cells * depth, slab * cells)
        high, low = halves_of(mixed)
        mixers.append(np.concatenate([high, high, low], axis=1))
    return np.stack(mixers)


def end_responses(field, order, place, groups):
    slab, width, length = field.shape
    depth, lanes = slab * groups, length // groups
    cells = divisor_of(width, 8, 16)
    mixers = mode_mixers(depth, groups, cells)
    return pl.pallas_call(
        functools.partial(ends_kernel, cells),
        grid_spec=pltpu.PrefetchScalarGridSpec(
            num_scalar_prefetch=1,
            grid=(groups // 2,),
            in_specs=[
                pl.BlockSpec((slab, width, 2 * lanes), lambda i, p: (0, 0, i)),
                pl.BlockSpec((1,) + mixers.shape[1:], lambda i, p: (p[0], 0, 0)),
                pl.BlockSpec((depth, 2 * lanes), lambda i, p: (0, i)),
                pl.BlockSpec(memory_space=pl.ANY),
            ],
            out_specs=pl.BlockSpec((2, 2, depth, lanes), lambda i, p: (i, 0, 0, 0)),
        ),
        out_shape=jax.ShapeDtypeStruct((groups, 2, depth, lanes), F32),
        compiler_params=params(),
        cost_estimate=cost(2 * mixers[0].size * length * (width // cells), field.size),
        name="end_responses",
    )(place, in_hbm(field), mixers, decay_table(length, depth), order)


def jumps_kernel(width, place_ref, ends_ref, ratio_ref, table_ref, order_ref, order_too_ref, out_ref):
    blocks = ends_ref.shape[0]
    here = place_ref[1]
    ratio = ratio_ref[0]
    block_power = power(ratio, width)
    gain = 1.0 / (1.0 - power(block_power, 2 * blocks))

    def end_of(block, side):
        mirrored = block >= blocks
        source = jnp.where(mirrored, 2 * blocks - 1 - block, block)
        return ends_ref[source, jnp.where(mirrored, 1 - side, side)]

    from_left = jnp.zeros_like(ratio)
    from_right = jnp.zeros_like(ratio)
    for k in range(2 * blocks):
        from_left = from_left * block_power + end_of((here + k) % (2 * blocks), 1)
        from_right = from_right * block_power + end_of((here + 2 * blocks - k) % (2 * blocks), 0)
    from_left = from_left * gain
    from_right = from_right * gain
    jump_left = from_left - (ends_ref[here, 0] + from_right * block_power)
    jump_right = (ends_ref[here, 1] + from_left * block_power) - from_right
    jump_left = jnp.where(place_ref[2] == 1, 0.0, (1.0 - ratio) * jump_left)
    jump_right = jnp.where(place_ref[3] == 1, 0.0, (1.0 - ratio) * jump_right)
    for side, jump in enumerate((jump_left, jump_right)):
        levels = jnp.dot(
            table_ref[...], jump, preferred_element_type=F32, precision=lax.Precision.HIGHEST
        )
        for g in range(out_ref.shape[0]):
            out_ref[g, side] = levels


def jumps(all_ends, orders, place, width, groups):
    _, _, depth, lanes = all_ends.shape
    ratio = decay_table(lanes * groups, depth).reshape(depth, groups, lanes).transpose(1, 0, 2)
    out = (groups, 2, depth, lanes)
    return pl.pallas_call(
        functools.partial(jumps_kernel, width),
        grid_spec=pltpu.PrefetchScalarGridSpec(
            num_scalar_prefetch=1,
            grid=(1,),
            in_specs=[
                fixed(all_ends.shape),
                pl.BlockSpec((1, depth, lanes), lambda i, p: (p[0], 0, 0)),
                fixed((depth, depth)),
                pl.BlockSpec(memory_space=pl.ANY),
                pl.BlockSpec(memory_space=pl.ANY),
            ],
            out_specs=fixed(out),
        ),
        out_shape=jax.ShapeDtypeStruct(out, F32),
        compiler_params=params(),
        cost_estimate=cost(20 * all_ends.size, all_ends.size),
        name="jumps",
    )(place, all_ends, ratio, level_table(depth).T.astype(np.float32), *orders)


def border_kernel(rows, place_ref, jump_ref, nu_ref, mu_ref, ends_ref, order_ref, out_ref, *refs):
    c_ref, prefix_ref, source_ref = refs
    _, _, depth, lanes = jump_ref.shape
    levels, width, _ = out_ref.shape
    aligned = (width // 2) % rows == 0
    for z in range(depth):
        left, right = jump_ref[0, 0, z : z + 1], jump_ref[0, 1, z : z + 1]
        source_ref[0, z] = jnp.broadcast_to(left - right, (8, lanes))
        source_ref[1, z] = jnp.broadcast_to(left + right, (8, lanes))

    def group(first, i, carry):
        at = pl.ds(pl.multiple_of(i * rows, rows), rows)
        sigma = nu_ref[at, 0:1] + mu_ref[...]
        if aligned:
            parity = (i * rows) // (width // 2)
        else:
            even = i * rows + lax.broadcasted_iota(jnp.int32, (rows, lanes), 0) < width // 2

        def source(z):
            if aligned:
                return jnp.concatenate([source_ref[parity, z]] * (rows // 8), axis=0)
            pair = [jnp.concatenate([source_ref[k, z]] * (rows // 8), axis=0) for k in range(2)]
            return jnp.where(even, *pair)

        zero = sigma * 0.0
        one = zero + 1.0
        if first < 0:
            c_ref[0], prefix_ref[0] = zero, zero
        c, slope, prefix = one, zero, zero
        for z in range(first + levels):
            prefix = prefix + c * source(z)
            slope = slope + sigma * c
            if z >= first:
                c_ref[z - first], prefix_ref[z - first] = c, prefix
            c = c + slope
        d, fall, suffix = one, one + one, zero
        for z in reversed(range(first + levels, depth)):
            suffix = suffix + d * source(z)
            fall = fall + sigma * d
            d = d + fall
        scale = slope * d + c_ref[levels - 1] * fall
        inverse = inverted(scale) * ends_ref[at, 0:1]
        for k in reversed(range(levels)):
            out_ref[k, at] = inverse * (d * prefix_ref[k] + c_ref[k] * suffix)
            if k and first + k >= 0:
                suffix = suffix + d * source(first + k)
                fall = fall + sigma * d
                d = d + fall
        return carry

    for slab_id in range(depth // (levels - 1)):
        first = slab_id * (levels - 1) - 1

        @pl.when(place_ref[0] == slab_id)
        def _(first=first):
            lax.fori_loop(0, width // rows, functools.partial(group, first), 0)


def border_solve(all_jumps, order, place, width, length, slab):
    groups, _, depth, lanes = all_jumps.shape
    rows = divisor_of(width, 8, 16)
    modes = spectral_order(width)
    nu = eigenvalues(width)[modes][:, None].astype(np.float32)
    mu = eigenvalues(length)[spectral_order(length)][None, :].astype(np.float32)
    ends = cosine_table(width)[modes][:, :1].astype(np.float32)
    return pl.pallas_call(
        functools.partial(border_kernel, rows),
        grid_spec=pltpu.PrefetchScalarGridSpec(
            num_scalar_prefetch=1,
            grid=(groups,),
            in_specs=[
                pl.BlockSpec((1, 2, depth, lanes), lambda i, p: (i, 0, 0, 0)),
                fixed(nu.shape),
                pl.BlockSpec((1, lanes), lambda i, p: (0, i)),
                fixed(ends.shape),
                pl.BlockSpec(memory_space=pl.ANY),
            ],
            out_specs=pl.BlockSpec((slab + 1, width, lanes), lambda i, p: (0, 0, i)),
            scratch_shapes=[pltpu.VMEM((slab + 1, rows, lanes), F32)] * 2
            + [pltpu.VMEM((2, depth, 8, lanes), F32)],
        ),
        out_shape=jax.ShapeDtypeStruct((slab + 1, width, length), F32),
        compiler_params=params(),
        cost_estimate=cost(20 * depth * width * length, (slab + 1) * width * length),
        name="border_solve",
    )(place, all_jumps, nu, mu, ends, order)


def block_dot(high_ref, low_ref, values):
    high, low = split(values)
    if values.shape[0] % 16 == 0:
        table = jnp.concatenate([high_ref[...], high_ref[...], low_ref[...]], axis=1)
        return dot(table, jnp.concatenate([high, low, high], axis=0))
    return dot(high_ref[...], high) + (dot(high_ref[...], low) + dot(low_ref[...], high))


def eliminate_kernel(place_ref, field_ref, ratio_ref, order_ref, high_ref, low_ref, *refs):
    modes_ref, last_ref, outer_ref, through_ref, weight_ref = refs
    t, steps = pl.program_id(0), pl.num_programs(0)
    modes = block_dot(high_ref, low_ref, field_ref[0])
    modes_ref[0] = modes
    ratio = ratio_ref[0]

    @pl.when(t == 0)
    def _():
        running = ratio * modes
        last_ref[...], outer_ref[...], weight_ref[...] = running, running, ratio

    @pl.when(t > 0)
    def _():
        running = ratio * (modes + last_ref[...])
        last_ref[...] = running

        @pl.when(t < steps - 1)
        def _():
            outer_ref[...] += weight_ref[...] * running
            weight_ref[...] *= ratio

        @pl.when(t == steps - 1)
        def _():
            through_ref[...] = weight_ref[...] * ratio


def eliminate(field, ratios, order, place):
    slab, width, length = field.shape
    lanes = length
    high, low = halves_of(cosine_table(width)[spectral_order(width)])
    plane = fixed((width, lanes))
    return pl.pallas_call(
        eliminate_kernel,
        grid_spec=pltpu.PrefetchScalarGridSpec(
            num_scalar_prefetch=1,
            grid=(slab,),
            in_specs=[
                pl.BlockSpec(
                    (1, width, lanes),
                    lambda t, p: (jnp.where(p[4] == 1, slab - 1 - t, t), 0, 0),
                ),
                pl.BlockSpec((1, width, lanes), lambda t, p: (t, 0, 0)),
                pl.BlockSpec(memory_space=pl.ANY),
                fixed(high.shape),
                fixed(low.shape),
            ],
            out_specs=[pl.BlockSpec((1, width, lanes), lambda t, p: (t, 0, 0)), plane, plane, plane],
            scratch_shapes=[pltpu.VMEM((width, lanes), F32)],
        ),
        out_shape=[hbm((slab, width, lanes))] + [hbm((width, lanes))] * 3,
        compiler_params=params(32),
        cost_estimate=cost(6 * width * field.size, 3 * field.size),
        name="eliminate",
    )(place, in_hbm(field), in_hbm(ratios), order, high, low)


def substitute_kernel(place_ref, modes_ref, ratio_ref, prev_ratio_ref, in_ref, next_ref, back_ref, border_ref, order_ref, high_ref, low_ref, out_ref, kept):
    slab = modes_ref.shape[0]
    upper = place_ref[4] == 1
    running = in_ref[...]
    for t in range(slab):
        running = ratio_ref[t] * (modes_ref[t] + running)
        kept[t] = running

    def emit(t, values):
        level = jnp.where(upper, slab - t, t + 1)
        out_ref[level] = block_dot(high_ref, low_ref, values + border_ref[level])

    beyond = next_ref[...] + back_ref[...]
    following = beyond
    for t in reversed(range(slab)):
        following = kept[t] + ratio_ref[t] * following
        emit(t, following)
    outside = in_ref[...] + prev_ratio_ref[0] * following
    values = jnp.where(upper, beyond, outside) + border_ref[0]
    out_ref[0] = block_dot(high_ref, low_ref, values)


def substitute(modes, ratios, incoming, following, back, border, order, place):
    slab, width, size = modes.shape
    lanes = divisor_of(size, 128, 384)
    per = size // lanes
    high, low = halves_of(cosine_table(width)[spectral_order(width)].T)
    plane = pl.BlockSpec((width, lanes), lambda i, p: (0, i))
    return pl.pallas_call(
        substitute_kernel,
        grid_spec=pltpu.PrefetchScalarGridSpec(
            num_scalar_prefetch=1,
            grid=(per,),
            in_specs=[
                pl.BlockSpec((slab, width, lanes), lambda i, p: (0, 0, i)),
                pl.BlockSpec((slab, width, lanes), lambda i, p: (0, 0, i)),
                pl.BlockSpec((1, width, lanes), lambda i, p: (slab, 0, i)),
                plane,
                plane,
                plane,
                pl.BlockSpec((slab + 1, width, lanes), lambda i, p: (0, 0, i)),
                pl.BlockSpec(memory_space=pl.ANY),
                fixed(high.shape),
                fixed(low.shape),
            ],
            out_specs=pl.BlockSpec((slab + 1, width, lanes), lambda i, p: (0, 0, i)),
            scratch_shapes=[pltpu.VMEM((slab, width, lanes), F32)],
        ),
        out_shape=hbm((slab + 1, width, size)),
        compiler_params=params(),
        cost_estimate=cost(9 * width * modes.size, 4 * modes.size),
        name="substitute",
    )(
        place, in_hbm(modes), in_hbm(ratios), in_hbm(ratios), incoming, following, back, border,
        order, high, low,
    )


def relay_kernel(last_ref, through_ref, in_ref, order_ref, out_ref):
    out_ref[...] = last_ref[...] + through_ref[...] * in_ref[...]


def row_tile(width):
    return divisor_of(width, 8, 48)


def relay(last, through, incoming, order):
    width, lanes = last.shape
    tile = row_tile(width)
    own = pl.BlockSpec((tile, lanes), lambda i: (i, 0))
    return pl.pallas_call(
        relay_kernel,
        grid=(width // tile,),
        in_specs=[
            own,
            own,
            own,
            pl.BlockSpec(memory_space=pl.ANY),
        ],
        out_specs=own,
        out_shape=jax.ShapeDtypeStruct(last.shape, F32),
        compiler_params=params(),
        cost_estimate=cost(2 * last.size, 4 * last.size),
        name="relay",
    )(in_hbm(last), in_hbm(through), incoming, order)


def turn_kernel(slab, place_ref, mine_ref, theirs_ref, in_ref, outer_ref, next_ref, ratios_ref, *refs):
    message_ref, follow_ref = refs[-2:]
    innermost = place_ref[5] == 1

    mine, theirs, follow = mine_ref[...], theirs_ref[...], next_ref[...]
    through = ratios_ref[0]
    weight, outer_in = through, through
    for t in range(1, slab):
        ratio = ratios_ref[t]
        through = through * ratio
        if t < slab - 1:
            outer_in = outer_in + weight * through
            weight = weight * ratio
    other = ratios_ref[slab + 1]
    meet = inverted(1.0 - ratio * other)
    inner = jnp.where(innermost, (mine + ratio * theirs) * meet, mine + ratio * follow)
    follow_ref[...] = jnp.where(innermost, (theirs + other * mine) * meet, follow)
    message_ref[...] = outer_ref[...] + outer_in * in_ref[...] + weight * inner


def turn(mine, theirs, incoming, outer, following, ratios, orders, place, chunk):
    width, lanes = mine.shape
    tile = row_tile(width)
    own = pl.BlockSpec((tile, lanes), lambda i, p: (i, 0))
    planes = ratios.shape[0]
    return pl.pallas_call(
        functools.partial(turn_kernel, planes - 2),
        grid_spec=pltpu.PrefetchScalarGridSpec(
            num_scalar_prefetch=1,
            grid=(width // tile,),
            in_specs=[own] * 5
            + [
                pl.BlockSpec((planes, tile, lanes), lambda i, p: (0, i, chunk)),
            ]
            + [pl.BlockSpec(memory_space=pl.ANY)] * len(orders),
            out_specs=[own] * 2,
        ),
        out_shape=[jax.ShapeDtypeStruct(mine.shape, F32), hbm(mine.shape)],
        compiler_params=params(),
        cost_estimate=cost(12 * mine.size, 12 * mine.size),
        name="turn",
    )(place, mine, theirs, incoming, in_hbm(outer), following, in_hbm(ratios), *orders)


def inverted(value):
    guess = pl.reciprocal(value, approx=True)
    guess = guess * (2.0 - value * guess)
    return guess * (2.0 - value * guess)


def sequence(sigma, upper, steps):
    value, slope = sigma * 0.0 + 1.0, sigma * 0.0 + (2.0 if upper else 0.0)
    for _ in range(steps):
        slope = slope + sigma * value
        value = value + slope
    return value, slope


def ratio_kernel(groups, lanes, place_ref, nu_ref, mu_ref, ratios_ref):
    planes, rows, length = ratios_ref.shape
    slab = planes - 2
    half = groups // 2

    def part(me, i, carry):
        upper = me >= half
        rank = groups - 1 - me if upper else me
        at = pl.ds(pl.multiple_of(i * lanes, lanes), lanes)
        sigma = nu_ref[...] + mu_ref[:, at]
        value, slope = sequence(sigma, upper, rank * slab)
        ratios_ref[slab, :, at] = (value - slope) * inverted(value) if rank else sigma * 0.0
        for t in range(slab):
            slope = slope + sigma * value
            following = value + slope
            ratios_ref[t, :, at] = value * inverted(following)
            value = following
        value, slope = sequence(sigma, not upper, half * slab)
        ratios_ref[slab + 1, :, at] = (value - slope) * inverted(value)
        return carry

    for me in range(groups):

        @pl.when(place_ref[0] == me)
        def _(me=me):
            lax.fori_loop(0, length // lanes, functools.partial(part, me), 0)


def pivots(width, length, slab, groups, place):
    rows = divisor_of(width, 8, 32)
    lanes = divisor_of(length, 128, 256)
    nu = eigenvalues(width)[spectral_order(width)][:, None].astype(np.float32)
    mu = eigenvalues(length)[spectral_order(length)][None, :].astype(np.float32)
    return pl.pallas_call(
        functools.partial(ratio_kernel, groups, lanes),
        grid_spec=pltpu.PrefetchScalarGridSpec(
            num_scalar_prefetch=1,
            grid=(width // rows,),
            in_specs=[pl.BlockSpec((rows, 1), lambda i, p: (i, 0)), fixed(mu.shape)],
            out_specs=pl.BlockSpec((slab + 2, rows, length), lambda i, p: (0, i, 0)),
        ),
        out_shape=hbm((slab + 2, width, length)),
        compiler_params=params(),
        cost_estimate=cost(120 * width * length, 6 * width * length),
        name="ratios",
    )(place, nu, mu)


def cut_kernel(d_top, f_top, d_first, f_first, d_last, f_last, top_ref, fraction_ref, first_ref, last_ref):
    slab = d_first.shape[0]
    top_ref[...] = d_top[...]
    fraction_ref[...] = f_top[...]
    first_ref[:slab] = d_first[:, 0:1]
    first_ref[slab:] = f_first[:, 0:1]
    last_ref[:slab] = d_last[:, 7:8]
    last_ref[slab:] = f_last[:, 7:8]


def cut_borders(direction, fraction):
    slab, width, lanes = direction.shape
    top = pl.BlockSpec((1, width, lanes), lambda i: (slab - 1, 0, 0))
    first = pl.BlockSpec((slab, 8, lanes), lambda i: (0, 0, 0))
    last = pl.BlockSpec((slab, 8, lanes), lambda i: (0, width // 8 - 1, 0))
    shapes = [(1, width, lanes)] * 2 + [(2 * slab, 1, lanes)] * 2
    direction, fraction = in_hbm(direction), in_hbm(fraction)
    return pl.pallas_call(
        cut_kernel,
        grid=(1,),
        in_specs=[top, top, first, first, last, last],
        out_specs=[fixed(shape) for shape in shapes],
        out_shape=[jax.ShapeDtypeStruct(shape, F32) for shape in shapes],
        compiler_params=params(),
        cost_estimate=cost(0, 4 * width * lanes),
        name="cut_borders",
    )(direction, fraction, direction, fraction, direction, fraction)


def neighbours(length):
    up = [(i, i + 1) for i in range(length - 1)]
    return up, [(j, i) for i, j in up]


def twice_inverse(total):
    guess = pl.reciprocal(total, approx=True)
    guess = guess * (2.0 - total * guess)
    return guess + guess


def operator_kernel(n_dots, n_kept, with_levels, place_ref, density_ref, *refs):
    if with_levels:
        (f_low, f_low_prev, f_low_next, f_ref, f_prev, f_next), refs = refs[:6], refs[6:]
    else:
        (f_ref, f_prev, f_next, f_below, f_below_too), refs = refs[:5], refs[5:]
    (f_lo, f_hi, d_ref, d_prev, d_next, d_below, d_lo, d_hi), refs = refs[:8], refs[8:]
    dot_refs = refs[:n_dots]
    face_ref, kept_ref, _, image_ref, out_sums_ref, out_face_ref = refs[n_dots : 6 + n_dots]
    field, dense, before_ref, sums_ref = refs[6 + n_dots :]
    slab, tile, lanes = image_ref.shape
    step, steps = pl.program_id(0), pl.num_programs(0)
    at_left = jnp.logical_and(place_ref[2] == 1, step == 0)
    at_right = jnp.logical_and(place_ref[3] == 1, step == steps - 1)
    at_bottom, at_top = place_ref[6] == 1, place_ref[7] == 1
    liquid, gas = density_ref[0], density_ref[1]

    def mixed(fraction):
        return fraction * gas + (1.0 - fraction) * liquid

    own = slice(8, 8 + tile)
    if with_levels:
        field[0:2, own] = f_low[...]
        field[2:, own] = f_ref[...]
    else:
        field[0:1, own] = f_below[...] + f_below_too[...]
        field[1:, own] = f_ref[...]
    dense[1:, own] = mixed(d_ref[...])
    dense[0:1, own] = mixed(d_below[...])

    @pl.when(step == 0)
    def _():
        field[1:, 7:8] = field[1:, 8:9] + f_lo[...] if with_levels else f_lo[...]
        dense[1:, 7:8] = mixed(d_lo[...])
        sums_ref[...] = jnp.zeros_like(sums_ref)

    @pl.when(step > 0)
    def _():
        if with_levels:
            field[1:2, 7:8] = f_low_prev[1:2, 7:8]
            field[2:, 7:8] = f_prev[:, 7:8]
        else:
            field[1:, 7:8] = f_prev[:, 7:8]
        dense[1:, 7:8] = mixed(d_prev[:, 7:8])

    @pl.when(step == steps - 1)
    def _():
        last_row = field[1:, 7 + tile : 8 + tile]
        field[1:, 8 + tile : 9 + tile] = last_row - f_hi[...] if with_levels else f_hi[...]
        dense[1:, 8 + tile : 9 + tile] = mixed(d_hi[...])

    @pl.when(step < steps - 1)
    def _():
        if with_levels:
            field[1:2, 8 + tile : 9 + tile] = f_low_next[1:2, 0:1]
            field[2:, 8 + tile : 9 + tile] = f_next[:, 0:1]
        else:
            field[1:, 8 + tile : 9 + tile] = f_next[:, 0:1]
        dense[1:, 8 + tile : 9 + tile] = mixed(d_next[:, 0:1])

    lane_ids = lax.broadcasted_iota(jnp.int32, (8, lanes), 1)
    row_ids = lax.broadcasted_iota(jnp.int32, (8, lanes), 0)
    has_right = (lane_ids < lanes - 1).astype(F32)

    def face(mid, rho, neighbour, rho_next):
        return twice_inverse(rho + rho_next) * (mid - neighbour)

    def next_row(ref, z, at, mid):
        following = ref[z, pl.ds(at + 8, 8)]
        return jnp.where(row_ids == 7, pltpu.roll(following, 7, 0), pltpu.roll(mid, 7, 0))

    def face_after(z, at, mid, rho):
        return face(mid, rho, next_row(field, z, at, mid), next_row(dense, z, at, rho))

    for level in range(slab):
        first = face_after(level + 1, 0, field[level + 1, 0:8], dense[level + 1, 0:8])
        before_ref[level] = jnp.where(at_left, 0.0, pltpu.roll(first, 1, 0))

    def rows(i, carry):
        at = pl.multiple_of(8 + 8 * i, 8)
        own = pl.ds(pl.multiple_of(8 * i, 8), 8)
        at_end = jnp.logical_and(at_right, i == tile // 8 - 1)
        mid, rho = field[0, pl.ds(at, 8)], dense[0, pl.ds(at, 8)]
        up, rho_up = field[1, pl.ds(at, 8)], dense[1, pl.ds(at, 8)]
        above = jnp.where(at_bottom, 0.0, face(mid, rho, up, rho_up))
        out_face_ref[0, own] = above
        totals = [mid * above] + [jnp.zeros((8, lanes), F32)] * n_dots
        if n_dots > 1:
            totals[-1] = jnp.where(at_bottom, 0.0, mid * face_ref[0, own])
        for level in range(slab):
            below = above
            mid, rho = up, rho_up
            if level < slab - 1:
                up, rho_up = field[level + 2, pl.ds(at, 8)], dense[level + 2, pl.ds(at, 8)]
                above = face(mid, rho, up, rho_up)
            else:
                above = jnp.where(at_top, twice_inverse(rho) * mid, 0.0)
            after = face_after(level + 1, at, mid, rho)
            after = jnp.where(jnp.logical_and(at_end, row_ids == 7), 0.0, after)
            shifted = pltpu.roll(after, 1, 0)
            before = jnp.where(row_ids == 0, before_ref[level], shifted)
            before_ref[level] = shifted
            right = has_right * face(
                mid, rho, pltpu.roll(mid, lanes - 1, 1), pltpu.roll(rho, lanes - 1, 1)
            )
            image = (above - below) + (after - before) + (right - pltpu.roll(right, 1, 1))
            image_ref[level, own] = image
            totals[0] = totals[0] + mid * image
            for k in range(n_dots):
                totals[k + 1] = totals[k + 1] + mid * dot_refs[k][level, own]
        for k in range(n_dots + 1):
            sums_ref[k] += totals[k]
        return carry

    lax.fori_loop(0, tile // 8, rows, 0)

    @pl.when(step == steps - 1)
    def _():
        group_ids = lax.broadcasted_iota(jnp.int32, (1, 128), 1) // 16
        packed = jnp.where(group_ids < n_kept, kept_ref[0], 0.0)
        for k in range(n_dots + 1):
            line = jnp.sum(sums_ref[k], axis=0, keepdims=True)
            line = sum(line[:, j : j + 128] for j in range(0, lanes, 128))
            for shift in (64, 32, 16):
                line = line + pltpu.roll(line, shift, 1)
            packed = jnp.where(group_ids == n_kept + k, line, packed)
        for k in range(out_sums_ref.shape[0]):
            out_sums_ref[k] = packed


def apply_operator(fields, belows, sides, fraction, border, density, others, face, kept, n_kept, copies, order, place, name):
    slab, width, lanes = fraction.shape
    with_levels = len(fields) > 1
    tile = divisor_of(width, 8, 48)
    per = tile // 8
    last = width // 8 - 1

    def triple(levels):
        return [
            pl.BlockSpec((levels, tile, lanes), lambda i, p: (0, i, 0)),
            pl.BlockSpec((levels, 8, lanes), lambda i, p: (0, jnp.maximum(i * per - 1, 0), 0)),
            pl.BlockSpec((levels, 8, lanes), lambda i, p: (0, jnp.minimum((i + 1) * per, last), 0)),
        ]

    plane = pl.BlockSpec((1, tile, lanes), lambda i, p: (0, i, 0))

    def borders(planes, *places):
        return [plane] * planes + [
            pl.BlockSpec((slab, 1, lanes), lambda i, p, k=k: (k, 0, 0)) for k in places
        ]

    own = pl.BlockSpec((slab, tile, lanes), lambda i, p: (0, i, 0))
    specs = [pl.BlockSpec(memory_space=pltpu.SMEM)]
    for field in fields:
        specs += triple(field.shape[0])
    specs += borders(0, 0, 1) if with_levels else borders(2, 0, 0)
    specs += triple(slab) + borders(1, 1, 1)
    specs += [own] * len(others)
    specs += [plane, fixed((1, 1, 128)), pl.BlockSpec(memory_space=pl.ANY)]
    planes = slab * (3 + len(others)) + 1
    operands = [field for field in fields for _ in range(3)] + ([] if with_levels else list(belows))
    return pl.pallas_call(
        functools.partial(operator_kernel, len(others), n_kept, with_levels),
        grid_spec=pltpu.PrefetchScalarGridSpec(
            num_scalar_prefetch=1,
            grid=(width // tile,),
            in_specs=specs,
            out_specs=[own, fixed((copies, 1, 128)), plane],
            scratch_shapes=[pltpu.VMEM((slab + 1, tile + 16, lanes), F32)] * 2
            + [
                pltpu.VMEM((slab, 8, lanes), F32),
                pltpu.VMEM((len(others) + 1, 8, lanes), F32),
            ],
        ),
        out_shape=[
            hbm((slab, width, lanes)),
            jax.ShapeDtypeStruct((copies, 1, 128), F32),
            hbm((1, width, lanes)),
        ],
        compiler_params=params(28),
        cost_estimate=cost(100 * slab * width * lanes, planes * width * lanes),
        name=name,
    )(
        place, density, *operands, *sides,
        fraction, fraction, fraction, *border, *others, face, kept, order,
    )


def update_kernel(sums_ref, low_ref, high_ref, direction_ref, solution_ref, residual_ref, old_ref, new_ref, old_face_ref, new_face_ref, *refs):
    solution_out, residual_out, direction_out = refs
    slab, _, lanes = direction_ref.shape
    packed = jnp.sum(sums_ref[...], axis=0)
    group_ids = lax.broadcasted_iota(jnp.int32, (1, 128), 1) // 16
    t0, t3, t4, t2, t1 = (
        jnp.broadcast_to(
            jnp.sum(jnp.where(group_ids == k, packed, 0.0), axis=1, keepdims=True), (1, 128)
        )
        for k in range(5)
    )
    t5 = t1
    conjugate = -t1 / t0
    along_r = t2 + conjugate * t3
    curvature = t4 + conjugate * (t1 + t5) + conjugate * conjugate * t0
    step_len = along_r / curvature
    conjugate = jnp.concatenate([conjugate] * (lanes // 128), axis=1)
    step_len = jnp.concatenate([step_len] * (lanes // 128), axis=1)
    for level in range(slab):
        precond = high_ref[level - 1] if level else low_ref[0]
        turned = precond + conjugate * direction_ref[level]
        direction_out[level] = turned
        solution_out[level] = solution_ref[level] + step_len * turned
        image = new_ref[level] + conjugate * old_ref[level]
        if level == slab - 1:
            image = image + (new_face_ref[0] + conjugate * old_face_ref[0])
        residual_out[level] = residual_ref[level] - step_len * image


def update(sums, precond_low, precond_high, direction, solution, residual, image_old, image_new, old_face, new_face):
    slab, width, lanes = direction.shape
    tile = divisor_of(width, 8, 24)
    own = pl.BlockSpec((slab, tile, lanes), lambda i: (0, i, 0))
    return pl.pallas_call(
        update_kernel,
        grid=(width // tile,),
        in_specs=[
            fixed(sums.shape),
            pl.BlockSpec((1, tile, lanes), lambda i: (1, i, 0)),
            pl.BlockSpec((slab - 1, tile, lanes), lambda i: (0, i, 0)),
        ]
        + [own] * 5
        + [pl.BlockSpec((1, tile, lanes), lambda i: (0, i, 0))] * 2,
        out_specs=[own] * 3,
        out_shape=[jax.ShapeDtypeStruct(direction.shape, F32)] * 3,
        compiler_params=params(28),
        cost_estimate=cost(10 * direction.size, 10 * direction.size),
        name="update",
    )(
        sums, in_hbm(precond_low), in_hbm(precond_high), in_hbm(direction), in_hbm(solution), in_hbm(residual),
        in_hbm(image_old), in_hbm(image_new), old_face, new_face,
    )


def body(solution, residual, direction, volume_fraction, density):
    slab, width, length = residual.shape
    groups, plane_parts = lax.axis_size("gz"), lax.axis_size("xy")
    half = groups // 2
    me, here = lax.axis_index("gz"), lax.axis_index("xy")
    upper = me >= half
    rank = jnp.where(upper, groups - 1 - me, me)
    innermost = rank == half - 1
    flags = [me, here, here == 0, here == plane_parts - 1, upper, innermost, me == 0, me == groups - 1]
    place = jnp.stack(flags + [rank]).astype(jnp.int32)
    scale = (2.0 / (1.0 / density[0] + 1.0 / density[1])).reshape(1)

    up, down = neighbours(groups)
    left, right = neighbours(plane_parts)[::-1]
    top, fraction_top, first_rows, last_rows = cut_borders(direction, volume_fraction)
    fraction_below = lax.ppermute(fraction_top, "gz", up)
    below = lax.ppermute(top, "gz", up[1:]) if up[1:] else jnp.zeros_like(top)
    sides = (lax.ppermute(last_rows, "xy", right), lax.ppermute(first_rows, "xy", left))

    spectral = forward_rows(residual.reshape(slab * width, length), scale)
    spectral = spectral.reshape(slab, width, length)
    ratios = pivots(width, length, slab, groups, place)
    inward = [[(s - 1, s), (groups - s, groups - 1 - s)] for s in range(1, half)]
    outward = [[(j, i) for i, j in pairs] for pairs in reversed(inward)]
    across = [(half - 1, half), (half, half - 1)]
    modes, last, outer, through = eliminate(spectral, ratios, fraction_below, place)
    zero = jnp.zeros_like(last)
    parts = end_responses(spectral, last, place, groups)
    late_top, parts = lax.optimization_barrier((top, parts))
    below_too = lax.ppermute(late_top, "gz", up[:1])
    ends = jnp.sum(lax.all_to_all(parts, "gz", 0, 0, tiled=True), axis=0)
    incoming, mine = zero, last
    for k, pairs in enumerate(inward):
        arrived = lax.ppermute(mine, "gz", pairs)
        incoming = incoming + arrived if k else arrived
        mine = relay(last, through, incoming, below)
    ends, mine = lax.optimization_barrier((ends, mine))
    all_ends = lax.all_to_all(
        jnp.broadcast_to(ends[None], (plane_parts,) + ends.shape), "xy", 0, 0, tiled=True
    )
    own_jumps = jumps(all_ends, sides, place, width, groups)
    all_jumps = lax.all_to_all(own_jumps, "gz", 0, 0, tiled=True)
    theirs = lax.ppermute(mine, "gz", across)
    orders = (below_too, all_jumps)
    message, following = turn(mine, theirs, incoming, outer, zero, ratios, orders, place, 0)
    back = zero
    for k, pairs in enumerate(outward):
        if k:
            message, following = turn(
                mine, theirs, incoming, outer, following + back, ratios, orders, place, 0
            )
        back = lax.ppermute(message, "gz", pairs)

    belows = (below, below_too)
    border = (fraction_below,) + sides
    nothing = jnp.zeros((1, 1, 128), F32)
    image_old, sums_old, old_face = apply_operator(
        [in_hbm(direction)], belows, sides, in_hbm(volume_fraction), border, density,
        [in_hbm(residual)], below, nothing, 0, 1, message, place, "image_old"
    )
    old_above = lax.ppermute(old_face, "gz", down)
    jumped = border_solve(all_jumps, message, place, width, length, slab)
    solved = substitute(modes, ratios, incoming, following, back, jumped, sums_old, place)
    precond_low, precond_high, jump_rows, new_face = inverse_rows(
        solved.reshape((slab + 1) * width, length), all_jumps, fraction_below,
        in_hbm(volume_fraction), density, place, width
    )
    new_above = lax.ppermute(new_face, "gz", down)
    image_new, sums, _ = apply_operator(
        [in_hbm(precond_low), in_hbm(precond_high)], belows, (jump_rows, jump_rows),
        in_hbm(volume_fraction), border, density, [in_hbm(residual), in_hbm(image_old)],
        in_hbm(old_face), sums_old, 2, groups * plane_parts, sums_old, place, "image_new"
    )
    gathered = lax.all_to_all(sums, ("gz", "xy"), 0, 0, tiled=True)
    new_solution, new_residual, new_direction = update(
        gathered, precond_low, precond_high, direction, solution, residual, image_old, image_new,
        old_above, new_above
    )
    return (new_solution, new_residual, new_direction)


def solution(mesh):
    placed = P("gz", "xy", None)
    return jax.shard_map(
        body,
        mesh=mesh,
        in_specs=(placed, placed, placed, placed, P()),
        out_specs=(placed, placed, placed),
        check_vma=False,
    )
```

```python
import functools

import jax
import jax.numpy as jnp
import numpy as np
from jax import lax
from jax.experimental import pallas as pl
from jax.experimental.pallas import tpu as pltpu
from jax.sharding import PartitionSpec as P

F32 = jnp.float32
BF16 = jnp.bfloat16
MIB = 1024 * 1024


def divisor_of(length, unit, largest):
    return max(t for t in range(unit, largest + 1, unit) if length % t == 0)


def halves_of(table):
    high = table.astype(BF16)
    low = (table - high.astype(np.float64)).astype(BF16)
    return high, low


def split(values):
    high = values.astype(BF16)
    return high, (values - high.astype(F32)).astype(BF16)


def dot(a, b):
    return jnp.dot(a, b, preferred_element_type=F32)


def dot3(a_high, a_low, b_high, b_low):
    return dot(a_high, b_high) + (dot(a_low, b_high) + dot(a_high, b_low))


def cosine_table(length):
    freq = np.arange(length)[:, None]
    cell = np.arange(length)[None, :]
    angles = np.pi / (2 * length) * (freq * (2 * cell + 1) % (4 * length))
    return np.where(freq == 0, np.sqrt(1.0 / length), np.sqrt(2.0 / length)) * np.cos(angles)


def spectral_order(length):
    return np.concatenate([np.arange(0, length, 2), np.arange(1, length, 2)])


def half_tables(length):
    half = length // 2
    return cosine_table(length)[spectral_order(length), :half].reshape(2, half, half)


def eigenvalues(length):
    return 4.0 * np.sin(np.pi * np.arange(length) / (2 * length)) ** 2


def level_table(depth):
    modes = np.arange(depth)[:, None]
    levels = np.arange(depth)[None, :]
    return np.sqrt(2.0 / depth) * np.cos(np.pi * (2 * modes + 1) * (2 * levels + 1) / (4 * depth))


def decay_table(length, depth):
    mu = eigenvalues(length)[spectral_order(length)]
    lam = 4.0 * np.sin(np.pi * (2 * np.arange(depth) + 1) / (4 * depth)) ** 2
    excess = lam[:, None] + mu[None, :]
    return (1.0 + excess / 2 - np.sqrt(excess + excess * excess / 4)).astype(np.float32)


def flip_matrix(size):
    return np.eye(size)[::-1].astype(BF16)


def flipped(high, low, flip):
    size = flip.shape[0]
    count = high.shape[1] // size
    blocks = []
    for i in range(count):
        part = slice((count - 1 - i) * size, (count - i) * size)
        blocks.append(dot(high[:, part], flip) + dot(low[:, part], flip))
    return jnp.concatenate(blocks, axis=1)


def power(base, exponent):
    result = None
    while exponent:
        if exponent & 1:
            result = base if result is None else result * base
        base = base * base
        exponent >>= 1
    return result


def fixed(shape):
    return pl.BlockSpec(shape, lambda *_: (0,) * len(shape))


def in_hbm(array):
    return pltpu.with_memory_space_constraint(array, pltpu.HBM)


def hbm(shape):
    return pltpu.HBM(shape, F32)


def params(mib=24):
    return pltpu.CompilerParams(vmem_limit_bytes=mib * MIB)


def cost(flops, count):
    return pl.CostEstimate(flops=int(flops) // 16, bytes_accessed=int(count) // 4, transcendentals=0)


def forward_kernel(scale_ref, rows_ref, high_ref, low_ref, flip_ref, out_ref):
    half = rows_ref.shape[1] // 2
    first, second = rows_ref[:, :half], rows_ref[:, half:]
    mirror = flipped(*split(second), flip_ref[...])
    scale = scale_ref[0]
    for parity, folded in enumerate((first + mirror, first - mirror)):
        out = dot3(*split(folded), high_ref[parity], low_ref[parity])
        out_ref[:, parity * half : (parity + 1) * half] = scale * out


def flip_of(half):
    return flip_matrix(256 if half % 256 == 0 else 128)


def forward_rows(rows, scale):
    count, length = rows.shape
    half = length // 2
    tile = divisor_of(count, 8, 256)
    high, low = halves_of(half_tables(length).transpose(0, 2, 1))
    flip = flip_of(half)
    return pl.pallas_call(
        forward_kernel,
        grid=(count // tile,),
        in_specs=[
            pl.BlockSpec(memory_space=pltpu.SMEM),
            pl.BlockSpec((tile, length), lambda i: (i, 0)),
            fixed(high.shape),
            fixed(low.shape),
            fixed(flip.shape),
        ],
        out_specs=pl.BlockSpec((tile, length), lambda i: (i, 0)),
        out_shape=hbm((count, length)),
        compiler_params=params(28),
        cost_estimate=cost(6 * count * length * half, 2 * count * length),
        name="forward_rows",
    )(scale, in_hbm(rows), in_hbm(high), in_hbm(low), flip)


def own_rows(place_ref, jump_ref, slab):
    rows = []
    for side in range(2):
        for level in range(slab):
            at = pl.ds(place_ref[0] * slab + level, 1)
            rows.append(jnp.concatenate([jump_ref[g, side, at] for g in range(jump_ref.shape[0])], axis=1))
    return jnp.concatenate(rows, axis=0)


def inverse_kernel(first_call, place_ref, density_ref, even_ref, odd_ref, high_ref, low_ref, flip_ref, *refs):
    half = even_ref.shape[1]

    def joined(even_part, odd_part):
        even = dot3(*split(even_part), high_ref[0], low_ref[0])
        odd = dot3(*split(odd_part), high_ref[1], low_ref[1])
        return even + odd, flipped(*split(even - odd), flip_ref[...])

    out_ref = refs[-3] if first_call else refs[0]
    first, second = joined(even_ref[...], odd_ref[...])
    out_ref[:, :half] = first
    out_ref[:, half:] = second
    if first_call:
        even_jump, odd_jump, below_ref, bottom_ref, _, out_rows_ref, face_ref = refs
        width, slab = face_ref.shape[1], out_rows_ref.shape[0] // 2
        pair = [own_rows(place_ref, jump, slab) for jump in (even_jump, odd_jump)]
        first, second = joined(*pair)
        out_rows_ref[:, 0, :half] = first
        out_rows_ref[:, 0, half:] = second
        liquid, gas = density_ref[0], density_ref[1]
        fractions = below_ref[0] + bottom_ref[0]
        total = fractions * gas + (2.0 - fractions) * liquid
        face_ref[0] = twice_inverse(total) * (out_ref[:width] - out_ref[width:])


def inverse_rows(solved, all_jumps, below, fraction, density, place, width):
    count, length = solved.shape
    half = length // 2
    slab = count // width - 1
    groups, _, depth, lanes = all_jumps.shape
    high, low = halves_of(half_tables(2 * half))
    flip = flip_of(half)
    tables = [fixed(high.shape)] * 2 + [fixed(flip.shape)]
    solved, high, low = in_hbm(solved), in_hbm(high), in_hbm(low)
    smem = pl.BlockSpec(memory_space=pltpu.SMEM)

    def jump(parity):
        return pl.BlockSpec((groups // 2, 2, depth, lanes), lambda i, p: (parity, 0, 0, 0))

    rows = [pl.BlockSpec((2 * width, half), lambda i, p, k=k: (0, k)) for k in range(2)]
    plane = fixed((1, width, 2 * half))
    lower, jump_rows, face = pl.pallas_call(
        functools.partial(inverse_kernel, True),
        grid_spec=pltpu.PrefetchScalarGridSpec(
            num_scalar_prefetch=1,
            grid=(1,),
            in_specs=[smem] + rows + tables + [jump(0), jump(1), plane, plane],
            out_specs=[fixed((2 * width, 2 * half)), fixed((2 * slab, 1, 2 * half)), plane],
        ),
        out_shape=[
            hbm((2 * width, 2 * half)),
            jax.ShapeDtypeStruct((2 * slab, 1, 2 * half), F32),
            jax.ShapeDtypeStruct((1, width, 2 * half), F32),
        ],
        compiler_params=params(36),
        cost_estimate=cost(28 * width * half * half, 8 * width * half),
        name="inverse_lower",
    )(place, density, solved, solved, high, low, flip, all_jumps, all_jumps, below, fraction)
    rest = (slab - 1) * width
    tile = max(t for t in (width, 2 * width, rest) if rest % t == 0 and t <= 384)
    skip = 2 * width // tile if 2 * width % tile == 0 else None
    if skip is None:
        tile, skip = width, 2
    rows = [pl.BlockSpec((tile, half), lambda i, p, k=k: (skip + i, k)) for k in range(2)]
    upper = pl.pallas_call(
        functools.partial(inverse_kernel, False),
        grid_spec=pltpu.PrefetchScalarGridSpec(
            num_scalar_prefetch=1,
            grid=(rest // tile,),
            in_specs=[smem] + rows + tables,
            out_specs=pl.BlockSpec((tile, 2 * half), lambda i, p: (i, 0)),
        ),
        out_shape=hbm((rest, 2 * half)),
        compiler_params=params(36),
        cost_estimate=cost(14 * rest * half * half, 4 * rest * half),
        name="inverse_upper",
    )(place, density, solved, solved, high, low, flip)
    return (
        lower.reshape(2, width, 2 * half), upper.reshape(slab - 1, width, 2 * half), jump_rows, face
    )


def ends_kernel(cells, place_ref, field_ref, mixer_ref, ratio_ref, out_ref):
    slab, width, lanes = field_ref.shape
    depth = ratio_ref.shape[0]
    ratio = ratio_ref[...]
    step_power = power(ratio, cells)

    def chunk(c, carry):
        right, left, weight = carry
        at = pl.multiple_of(c * cells, cells)
        stacked = field_ref[:, pl.ds(at, cells), :].reshape(slab * cells, lanes)
        high, low = split(stacked)
        modes = dot(mixer_ref[0], jnp.concatenate([high, low, high], axis=0))
        inner = modes[(cells - 1) * depth :]
        for k in reversed(range(cells - 1)):
            inner = inner * ratio + modes[k * depth : (k + 1) * depth]
        for k in range(cells):
            right = right * ratio + modes[k * depth : (k + 1) * depth]
        return right, left + weight * inner, weight * step_power

    zero = jnp.zeros((depth, lanes), F32)
    right, left, _ = lax.fori_loop(0, width // cells, chunk, (zero, zero, zero + 1.0), unroll=2)
    gain = ratio / (1.0 - ratio * ratio)
    left, right = left * gain, right * gain
    per, _, _, part = out_ref.shape
    for g in range(per):
        out_ref[g, 0] = left[:, g * part : (g + 1) * part]
        out_ref[g, 1] = right[:, g * part : (g + 1) * part]


def mode_mixers(depth, groups, cells):
    table = level_table(depth)
    slab = depth // groups
    mixers = []
    for me in range(groups):
        own = table[:, me * slab : (me + 1) * slab]
        mixed = np.einsum("kz,ab->akzb", own, np.eye(cells)).reshape(cells * depth, slab * cells)
        high, low = halves_of(mixed)
        mixers.append(np.concatenate([high, high, low], axis=1))
    return np.stack(mixers)


def end_responses(field, place, groups):
    slab, width, length = field.shape
    depth, lanes = slab * groups, length // groups
    cells = divisor_of(width, 8, 16)
    mixers = mode_mixers(depth, groups, cells)
    return pl.pallas_call(
        functools.partial(ends_kernel, cells),
        grid_spec=pltpu.PrefetchScalarGridSpec(
            num_scalar_prefetch=1,
            grid=(groups // 2,),
            in_specs=[
                pl.BlockSpec((slab, width, 2 * lanes), lambda i, p: (0, 0, i)),
                pl.BlockSpec((1,) + mixers.shape[1:], lambda i, p: (p[0], 0, 0)),
                pl.BlockSpec((depth, 2 * lanes), lambda i, p: (0, i)),
            ],
            out_specs=pl.BlockSpec((2, 2, depth, lanes), lambda i, p: (i, 0, 0, 0)),
        ),
        out_shape=jax.ShapeDtypeStruct((groups, 2, depth, lanes), F32),
        compiler_params=params(),
        cost_estimate=cost(2 * mixers[0].size * length * (width // cells), field.size),
        name="end_responses",
    )(place, in_hbm(field), mixers, decay_table(length, depth))


def jumps_kernel(width, place_ref, ends_ref, ratio_ref, table_ref, out_ref):
    blocks = ends_ref.shape[0]
    here = place_ref[1]
    ratio = ratio_ref[0]
    block_power = power(ratio, width)
    gain = 1.0 / (1.0 - power(block_power, 2 * blocks))

    def end_of(block, side):
        mirrored = block >= blocks
        source = jnp.where(mirrored, 2 * blocks - 1 - block, block)
        return ends_ref[source, jnp.where(mirrored, 1 - side, side)]

    from_left = jnp.zeros_like(ratio)
    from_right = jnp.zeros_like(ratio)
    for k in range(2 * blocks):
        from_left = from_left * block_power + end_of((here + k) % (2 * blocks), 1)
        from_right = from_right * block_power + end_of((here + 2 * blocks - k) % (2 * blocks), 0)
    from_left = from_left * gain
    from_right = from_right * gain
    jump_left = from_left - (ends_ref[here, 0] + from_right * block_power)
    jump_right = (ends_ref[here, 1] + from_left * block_power) - from_right
    jump_left = jnp.where(place_ref[2] == 1, 0.0, (1.0 - ratio) * jump_left)
    jump_right = jnp.where(place_ref[3] == 1, 0.0, (1.0 - ratio) * jump_right)
    for side, jump in enumerate((jump_left, jump_right)):
        levels = jnp.dot(
            table_ref[...], jump, preferred_element_type=F32, precision=lax.Precision.HIGHEST
        )
        for g in range(out_ref.shape[0]):
            out_ref[g, side] = levels


def jumps(all_ends, place, width, groups):
    _, _, depth, lanes = all_ends.shape
    ratio = decay_table(lanes * groups, depth).reshape(depth, groups, lanes).transpose(1, 0, 2)
    out = (groups, 2, depth, lanes)
    return pl.pallas_call(
        functools.partial(jumps_kernel, width),
        grid_spec=pltpu.PrefetchScalarGridSpec(
            num_scalar_prefetch=1,
            grid=(1,),
            in_specs=[
                fixed(all_ends.shape),
                pl.BlockSpec((1, depth, lanes), lambda i, p: (p[0], 0, 0)),
                fixed((depth, depth)),
            ],
            out_specs=fixed(out),
        ),
        out_shape=jax.ShapeDtypeStruct(out, F32),
        compiler_params=params(),
        cost_estimate=cost(20 * all_ends.size, all_ends.size),
        name="jumps",
    )(place, all_ends, ratio, level_table(depth).T.astype(np.float32))


def border_kernel(rows, place_ref, jump_ref, nu_ref, mu_ref, ends_ref, order_ref, out_ref, *refs):
    c_ref, prefix_ref, source_ref = refs
    _, _, depth, lanes = jump_ref.shape
    levels, width, _ = out_ref.shape
    aligned = (width // 2) % rows == 0
    for z in range(depth):
        left, right = jump_ref[0, 0, z : z + 1], jump_ref[0, 1, z : z + 1]
        source_ref[0, z] = jnp.broadcast_to(left - right, (8, lanes))
        source_ref[1, z] = jnp.broadcast_to(left + right, (8, lanes))

    def group(first, i, carry):
        at = pl.ds(pl.multiple_of(i * rows, rows), rows)
        sigma = nu_ref[at, 0:1] + mu_ref[...]
        if aligned:
            parity = (i * rows) // (width // 2)
        else:
            even = i * rows + lax.broadcasted_iota(jnp.int32, (rows, lanes), 0) < width // 2

        def source(z):
            if aligned:
                return jnp.concatenate([source_ref[parity, z]] * (rows // 8), axis=0)
            pair = [jnp.concatenate([source_ref[k, z]] * (rows // 8), axis=0) for k in range(2)]
            return jnp.where(even, *pair)

        zero = sigma * 0.0
        one = zero + 1.0
        if first < 0:
            c_ref[0], prefix_ref[0] = zero, zero
        c, slope, prefix = one, zero, zero
        for z in range(first + levels):
            prefix = prefix + c * source(z)
            slope = slope + sigma * c
            if z >= first:
                c_ref[z - first], prefix_ref[z - first] = c, prefix
            c = c + slope
        d, fall, suffix = one, one + one, zero
        for z in reversed(range(first + levels, depth)):
            suffix = suffix + d * source(z)
            fall = fall + sigma * d
            d = d + fall
        scale = slope * d + c_ref[levels - 1] * fall
        inverse = inverted(scale) * ends_ref[at, 0:1]
        for k in reversed(range(levels)):
            out_ref[k, at] = inverse * (d * prefix_ref[k] + c_ref[k] * suffix)
            if k and first + k >= 0:
                suffix = suffix + d * source(first + k)
                fall = fall + sigma * d
                d = d + fall
        return carry

    for slab_id in range(depth // (levels - 1)):
        first = slab_id * (levels - 1) - 1

        @pl.when(place_ref[0] == slab_id)
        def _(first=first):
            lax.fori_loop(0, width // rows, functools.partial(group, first), 0)


def border_solve(all_jumps, order, place, width, length, slab):
    groups, _, depth, lanes = all_jumps.shape
    rows = divisor_of(width, 8, 16)
    modes = spectral_order(width)
    nu = eigenvalues(width)[modes][:, None].astype(np.float32)
    mu = eigenvalues(length)[spectral_order(length)][None, :].astype(np.float32)
    ends = cosine_table(width)[modes][:, :1].astype(np.float32)
    return pl.pallas_call(
        functools.partial(border_kernel, rows),
        grid_spec=pltpu.PrefetchScalarGridSpec(
            num_scalar_prefetch=1,
            grid=(groups,),
            in_specs=[
                pl.BlockSpec((1, 2, depth, lanes), lambda i, p: (i, 0, 0, 0)),
                fixed(nu.shape),
                pl.BlockSpec((1, lanes), lambda i, p: (0, i)),
                fixed(ends.shape),
                pl.BlockSpec(memory_space=pl.ANY),
            ],
            out_specs=pl.BlockSpec((slab + 1, width, lanes), lambda i, p: (0, 0, i)),
            scratch_shapes=[pltpu.VMEM((slab + 1, rows, lanes), F32)] * 2
            + [pltpu.VMEM((2, depth, 8, lanes), F32)],
        ),
        out_shape=jax.ShapeDtypeStruct((slab + 1, width, length), F32),
        compiler_params=params(),
        cost_estimate=cost(20 * depth * width * length, (slab + 1) * width * length),
        name="border_solve",
    )(place, all_jumps, nu, mu, ends, order)


def block_dot(high_ref, low_ref, values):
    high, low = split(values)
    if values.shape[0] % 16 == 0:
        table = jnp.concatenate([high_ref[...], high_ref[...], low_ref[...]], axis=1)
        return dot(table, jnp.concatenate([high, low, high], axis=0))
    return dot(high_ref[...], high) + (dot(high_ref[...], low) + dot(low_ref[...], high))


def eliminate_kernel(place_ref, field_ref, ratio_ref, high_ref, low_ref, *refs):
    modes_ref, last_ref, outer_ref, through_ref, weight_ref = refs[-5:]
    t, steps = pl.program_id(0), pl.num_programs(0)
    modes = block_dot(high_ref, low_ref, field_ref[0])
    modes_ref[0] = modes
    ratio = ratio_ref[0]

    @pl.when(t == 0)
    def _():
        running = ratio * modes
        last_ref[...], outer_ref[...], weight_ref[...] = running, running, ratio

    @pl.when(t > 0)
    def _():
        running = ratio * (modes + last_ref[...])
        last_ref[...] = running

        @pl.when(t < steps - 1)
        def _():
            outer_ref[...] += weight_ref[...] * running
            weight_ref[...] *= ratio

        @pl.when(t == steps - 1)
        def _():
            through_ref[...] = weight_ref[...] * ratio


def eliminate(field, ratios, orders, place):
    slab, width, length = field.shape
    lanes = length
    high, low = halves_of(cosine_table(width)[spectral_order(width)])
    plane = fixed((width, lanes))
    return pl.pallas_call(
        eliminate_kernel,
        grid_spec=pltpu.PrefetchScalarGridSpec(
            num_scalar_prefetch=1,
            grid=(slab,),
            in_specs=[
                pl.BlockSpec(
                    (1, width, lanes),
                    lambda t, p: (jnp.where(p[4] == 1, slab - 1 - t, t), 0, 0),
                ),
                pl.BlockSpec((1, width, lanes), lambda t, p: (t, 0, 0)),
                fixed(high.shape),
                fixed(low.shape),
            ]
            + [pl.BlockSpec(memory_space=pl.ANY)] * len(orders),
            out_specs=[pl.BlockSpec((1, width, lanes), lambda t, p: (t, 0, 0)), plane, plane, plane],
            scratch_shapes=[pltpu.VMEM((width, lanes), F32)],
        ),
        out_shape=[hbm((slab, width, lanes))] + [hbm((width, lanes))] * 3,
        compiler_params=params(32),
        cost_estimate=cost(6 * width * field.size, 3 * field.size),
        name="eliminate",
    )(place, in_hbm(field), in_hbm(ratios), high, low, *orders)


def substitute_kernel(place_ref, modes_ref, ratio_ref, prev_ratio_ref, in_ref, next_ref, back_ref, border_ref, order_ref, high_ref, low_ref, out_ref, kept):
    slab = modes_ref.shape[0]
    upper = place_ref[4] == 1
    running = in_ref[...]
    for t in range(slab):
        running = ratio_ref[t] * (modes_ref[t] + running)
        kept[t] = running

    def emit(t, values):
        level = jnp.where(upper, slab - t, t + 1)
        out_ref[level] = block_dot(high_ref, low_ref, values + border_ref[level])

    beyond = next_ref[...] + back_ref[...]
    following = beyond
    for t in reversed(range(slab)):
        following = kept[t] + ratio_ref[t] * following
        emit(t, following)
    outside = in_ref[...] + prev_ratio_ref[0] * following
    values = jnp.where(upper, beyond, outside) + border_ref[0]
    out_ref[0] = block_dot(high_ref, low_ref, values)


def substitute(modes, ratios, incoming, following, back, border, order, place):
    slab, width, size = modes.shape
    lanes = divisor_of(size, 128, 384)
    per = size // lanes
    high, low = halves_of(cosine_table(width)[spectral_order(width)].T)
    plane = pl.BlockSpec((width, lanes), lambda i, p: (0, i))
    return pl.pallas_call(
        substitute_kernel,
        grid_spec=pltpu.PrefetchScalarGridSpec(
            num_scalar_prefetch=1,
            grid=(per,),
            in_specs=[
                pl.BlockSpec((slab, width, lanes), lambda i, p: (0, 0, i)),
                pl.BlockSpec((slab, width, lanes), lambda i, p: (0, 0, i)),
                pl.BlockSpec((1, width, lanes), lambda i, p: (slab, 0, i)),
                plane,
                plane,
                plane,
                pl.BlockSpec((slab + 1, width, lanes), lambda i, p: (0, 0, i)),
                pl.BlockSpec(memory_space=pl.ANY),
                fixed(high.shape),
                fixed(low.shape),
            ],
            out_specs=pl.BlockSpec((slab + 1, width, lanes), lambda i, p: (0, 0, i)),
            scratch_shapes=[pltpu.VMEM((slab, width, lanes), F32)],
        ),
        out_shape=hbm((slab + 1, width, size)),
        compiler_params=params(),
        cost_estimate=cost(9 * width * modes.size, 4 * modes.size),
        name="substitute",
    )(
        place, in_hbm(modes), in_hbm(ratios), in_hbm(ratios), incoming, following, back, border,
        order, high, low,
    )


def relay_kernel(last_ref, through_ref, in_ref, *refs):
    out_ref = refs[-1]
    out_ref[...] = last_ref[...] + through_ref[...] * in_ref[...]


def row_tile(width):
    return divisor_of(width, 8, 48)


def relay(last, through, incoming, orders):
    width, lanes = last.shape
    tile = row_tile(width)
    own = pl.BlockSpec((tile, lanes), lambda i: (i, 0))
    return pl.pallas_call(
        relay_kernel,
        grid=(width // tile,),
        in_specs=[
            own,
            own,
            own,
        ]
        + [pl.BlockSpec(memory_space=pl.ANY)] * len(orders),
        out_specs=own,
        out_shape=jax.ShapeDtypeStruct(last.shape, F32),
        compiler_params=params(),
        cost_estimate=cost(2 * last.size, 4 * last.size),
        name="relay",
    )(in_hbm(last), in_hbm(through), incoming, *orders)


def turn_kernel(slab, place_ref, mine_ref, theirs_ref, in_ref, outer_ref, next_ref, ratios_ref, *refs):
    message_ref, follow_ref = refs[-2:]
    innermost = place_ref[5] == 1

    mine, theirs, follow = mine_ref[...], theirs_ref[...], next_ref[...]
    through = ratios_ref[0]
    weight, outer_in = through, through
    for t in range(1, slab):
        ratio = ratios_ref[t]
        through = through * ratio
        if t < slab - 1:
            outer_in = outer_in + weight * through
            weight = weight * ratio
    other = ratios_ref[slab + 1]
    meet = inverted(1.0 - ratio * other)
    inner = jnp.where(innermost, (mine + ratio * theirs) * meet, mine + ratio * follow)
    follow_ref[...] = jnp.where(innermost, (theirs + other * mine) * meet, follow)
    message_ref[...] = outer_ref[...] + outer_in * in_ref[...] + weight * inner


def turn(mine, theirs, incoming, outer, following, ratios, orders, place, chunk):
    width, lanes = mine.shape
    tile = row_tile(width)
    own = pl.BlockSpec((tile, lanes), lambda i, p: (i, 0))
    planes = ratios.shape[0]
    return pl.pallas_call(
        functools.partial(turn_kernel, planes - 2),
        grid_spec=pltpu.PrefetchScalarGridSpec(
            num_scalar_prefetch=1,
            grid=(width // tile,),
            in_specs=[own] * 5
            + [
                pl.BlockSpec((planes, tile, lanes), lambda i, p: (0, i, chunk)),
            ]
            + [pl.BlockSpec(memory_space=pl.ANY)] * len(orders),
            out_specs=[own] * 2,
        ),
        out_shape=[jax.ShapeDtypeStruct(mine.shape, F32), hbm(mine.shape)],
        compiler_params=params(),
        cost_estimate=cost(12 * mine.size, 12 * mine.size),
        name="turn",
    )(place, mine, theirs, incoming, in_hbm(outer), following, in_hbm(ratios), *orders)


def inverted(value):
    guess = pl.reciprocal(value, approx=True)
    guess = guess * (2.0 - value * guess)
    return guess * (2.0 - value * guess)


def sequence(sigma, upper, steps):
    value, slope = sigma * 0.0 + 1.0, sigma * 0.0 + (2.0 if upper else 0.0)
    for _ in range(steps):
        slope = slope + sigma * value
        value = value + slope
    return value, slope


def ratio_kernel(groups, lanes, place_ref, nu_ref, mu_ref, ratios_ref):
    planes, rows, length = ratios_ref.shape
    slab = planes - 2
    half = groups // 2

    def part(me, i, carry):
        upper = me >= half
        rank = groups - 1 - me if upper else me
        at = pl.ds(pl.multiple_of(i * lanes, lanes), lanes)
        sigma = nu_ref[...] + mu_ref[:, at]
        value, slope = sequence(sigma, upper, rank * slab)
        ratios_ref[slab, :, at] = (value - slope) * inverted(value) if rank else sigma * 0.0
        for t in range(slab):
            slope = slope + sigma * value
            following = value + slope
            ratios_ref[t, :, at] = value * inverted(following)
            value = following
        value, slope = sequence(sigma, not upper, half * slab)
        ratios_ref[slab + 1, :, at] = (value - slope) * inverted(value)
        return carry

    for me in range(groups):

        @pl.when(place_ref[0] == me)
        def _(me=me):
            lax.fori_loop(0, length // lanes, functools.partial(part, me), 0)


def pivots(width, length, slab, groups, place):
    rows = divisor_of(width, 8, 32)
    lanes = divisor_of(length, 128, 256)
    nu = eigenvalues(width)[spectral_order(width)][:, None].astype(np.float32)
    mu = eigenvalues(length)[spectral_order(length)][None, :].astype(np.float32)
    return pl.pallas_call(
        functools.partial(ratio_kernel, groups, lanes),
        grid_spec=pltpu.PrefetchScalarGridSpec(
            num_scalar_prefetch=1,
            grid=(width // rows,),
            in_specs=[pl.BlockSpec((rows, 1), lambda i, p: (i, 0)), fixed(mu.shape)],
            out_specs=pl.BlockSpec((slab + 2, rows, length), lambda i, p: (0, i, 0)),
        ),
        out_shape=hbm((slab + 2, width, length)),
        compiler_params=params(),
        cost_estimate=cost(120 * width * length, 6 * width * length),
        name="ratios",
    )(place, nu, mu)


def cut_kernel(d_top, f_top, d_first, f_first, d_last, f_last, top_ref, fraction_ref, first_ref, last_ref):
    slab = d_first.shape[0]
    top_ref[...] = d_top[...]
    fraction_ref[...] = f_top[...]
    first_ref[:slab] = d_first[:, 0:1]
    first_ref[slab:] = f_first[:, 0:1]
    last_ref[:slab] = d_last[:, 7:8]
    last_ref[slab:] = f_last[:, 7:8]


def cut_borders(direction, fraction):
    slab, width, lanes = direction.shape
    top = pl.BlockSpec((1, width, lanes), lambda i: (slab - 1, 0, 0))
    first = pl.BlockSpec((slab, 8, lanes), lambda i: (0, 0, 0))
    last = pl.BlockSpec((slab, 8, lanes), lambda i: (0, width // 8 - 1, 0))
    shapes = [(1, width, lanes)] * 2 + [(2 * slab, 1, lanes)] * 2
    direction, fraction = in_hbm(direction), in_hbm(fraction)
    return pl.pallas_call(
        cut_kernel,
        grid=(1,),
        in_specs=[top, top, first, first, last, last],
        out_specs=[fixed(shape) for shape in shapes],
        out_shape=[jax.ShapeDtypeStruct(shape, F32) for shape in shapes],
        compiler_params=params(),
        cost_estimate=cost(0, 4 * width * lanes),
        name="cut_borders",
    )(direction, fraction, direction, fraction, direction, fraction)


def neighbours(length):
    up = [(i, i + 1) for i in range(length - 1)]
    return up, [(j, i) for i, j in up]


def twice_inverse(total):
    guess = pl.reciprocal(total, approx=True)
    guess = guess * (2.0 - total * guess)
    return guess + guess


def next_row(following, mid):
    row_ids = lax.broadcasted_iota(jnp.int32, mid.shape, 0)
    return jnp.where(row_ids == 7, pltpu.roll(following, 7, 0), pltpu.roll(mid, 7, 0))


def previous_row(carried_ref, level, after):
    row_ids = lax.broadcasted_iota(jnp.int32, after.shape, 0)
    shifted = pltpu.roll(after, 1, 0)
    before = jnp.where(row_ids == 0, carried_ref[level], shifted)
    carried_ref[level] = shifted
    return before


def pack_sums(out_ref, kept, first, sums_ref):
    group_ids = lax.broadcasted_iota(jnp.int32, (1, 128), 1) // 16
    packed = kept
    for k in range(sums_ref.shape[0]):
        line = jnp.sum(sums_ref[k], axis=0, keepdims=True)
        line = sum(line[:, j : j + 128] for j in range(0, line.shape[1], 128))
        for shift in (64, 32, 16):
            line = line + pltpu.roll(line, shift, 1)
        packed = jnp.where(group_ids == first + k, line, packed)
    for k in range(out_ref.shape[0]):
        out_ref[k] = packed


def old_image_kernel(
    place_ref, density_ref, f_ref, f_prev, f_next, f_below, f_below_too, f_lo, f_hi,
    d_ref, d_prev, d_next, d_below, d_lo, d_hi, residual_ref, order_ref,
    image_ref, out_sums_ref, out_face_ref, z_ref, x_ref, x_first_ref, y_ref,
    field, dense, before_ref, sums_ref,
):
    slab, tile, lanes = image_ref.shape
    step, steps = pl.program_id(0), pl.num_programs(0)
    at_left = jnp.logical_and(place_ref[2] == 1, step == 0)
    at_right = jnp.logical_and(place_ref[3] == 1, step == steps - 1)
    at_bottom, at_top = place_ref[6] == 1, place_ref[7] == 1
    liquid, gas = density_ref[0], density_ref[1]

    def mixed(fraction):
        return fraction * gas + (1.0 - fraction) * liquid

    own = slice(8, 8 + tile)
    field[0:1, own] = f_below[...] + f_below_too[...]
    field[1:, own] = f_ref[...]
    dense[1:, own] = mixed(d_ref[...])
    dense[0:1, own] = mixed(d_below[...])

    @pl.when(step == 0)
    def _():
        field[1:, 7:8] = f_lo[...]
        dense[1:, 7:8] = mixed(d_lo[...])
        sums_ref[...] = jnp.zeros_like(sums_ref)

    @pl.when(step > 0)
    def _():
        field[1:, 7:8] = f_prev[:, 7:8]
        dense[1:, 7:8] = mixed(d_prev[:, 7:8])

    @pl.when(step == steps - 1)
    def _():
        field[1:, 8 + tile : 9 + tile] = f_hi[...]
        dense[1:, 8 + tile : 9 + tile] = mixed(d_hi[...])

    @pl.when(step < steps - 1)
    def _():
        field[1:, 8 + tile : 9 + tile] = f_next[:, 0:1]
        dense[1:, 8 + tile : 9 + tile] = mixed(d_next[:, 0:1])

    lane_ids = lax.broadcasted_iota(jnp.int32, (8, lanes), 1)
    row_ids = lax.broadcasted_iota(jnp.int32, (8, lanes), 0)
    has_right = (lane_ids < lanes - 1).astype(F32)

    def after_faces(z, at, mid, rho):
        below = pl.ds(at + 8, 8)
        coefficient = twice_inverse(rho + next_row(dense[z, below], rho))
        return coefficient, mid - next_row(field[z, below], mid)

    for level in range(slab):
        coefficient, drop = after_faces(level + 1, 0, field[level + 1, 0:8], dense[level + 1, 0:8])
        coefficient = jnp.where(at_left, 0.0, coefficient)
        before_ref[level] = pltpu.roll(jnp.where(at_left, 0.0, coefficient * drop), 1, 0)

        @pl.when(step == 0)
        def _(level=level, coefficient=coefficient):
            x_first_ref[level] = jnp.where(row_ids == 7, coefficient, 0.0)

    def rows(i, carry):
        at = pl.multiple_of(8 + 8 * i, 8)
        here = pl.ds(at, 8)
        own = pl.ds(pl.multiple_of(8 * i, 8), 8)
        at_end = jnp.logical_and(at_right, i == tile // 8 - 1)
        mid, rho = field[0, here], dense[0, here]
        up, rho_up = field[1, here], dense[1, here]
        coefficient = jnp.where(at_bottom, 0.0, twice_inverse(rho + rho_up))
        z_ref[0, own] = coefficient
        above = coefficient * (mid - up)
        out_face_ref[0, own] = above
        totals = [mid * above, jnp.zeros((8, lanes), F32)]
        for level in range(slab):
            below = above
            mid, rho = up, rho_up
            if level < slab - 1:
                up, rho_up = field[level + 2, here], dense[level + 2, here]
                coefficient = twice_inverse(rho + rho_up)
                above = coefficient * (mid - up)
            else:
                coefficient = jnp.where(at_top, twice_inverse(rho), 0.0)
                above = coefficient * mid
            z_ref[level + 1, own] = coefficient
            coefficient, drop = after_faces(level + 1, at, mid, rho)
            coefficient = jnp.where(jnp.logical_and(at_end, row_ids == 7), 0.0, coefficient)
            x_ref[level, own] = coefficient
            after = coefficient * drop
            before = previous_row(before_ref, level, after)
            coefficient = has_right * twice_inverse(rho + pltpu.roll(rho, lanes - 1, 1))
            y_ref[level, own] = coefficient
            right = coefficient * (mid - pltpu.roll(mid, lanes - 1, 1))
            image = (above - below) + (after - before) + (right - pltpu.roll(right, 1, 1))
            image_ref[level, own] = image
            totals[0] = totals[0] + mid * image
            totals[1] = totals[1] + mid * residual_ref[level, own]
        for k in range(2):
            sums_ref[k] += totals[k]
        return carry

    lax.fori_loop(0, tile // 8, rows, 0)

    @pl.when(step == steps - 1)
    def _():
        pack_sums(out_sums_ref, jnp.zeros((1, 128), F32), 0, sums_ref)


def stencil_tile(width):
    return divisor_of(width, 8, 48)


def old_image(direction, belows, sides, fraction, fraction_below, density, residual, order, place):
    slab, width, lanes = fraction.shape
    tile = stencil_tile(width)
    per = tile // 8
    last = width // 8 - 1
    plane = pl.BlockSpec((1, tile, lanes), lambda i, p: (0, i, 0))
    own = pl.BlockSpec((slab, tile, lanes), lambda i, p: (0, i, 0))
    triple = [
        own,
        pl.BlockSpec((slab, 8, lanes), lambda i, p: (0, jnp.maximum(i * per - 1, 0), 0)),
        pl.BlockSpec((slab, 8, lanes), lambda i, p: (0, jnp.minimum((i + 1) * per, last), 0)),
    ]

    def side(k):
        return [pl.BlockSpec((slab, 1, lanes), lambda i, p: (k, 0, 0))] * 2

    specs = [pl.BlockSpec(memory_space=pltpu.SMEM)] + triple + [plane] * 2 + side(0)
    specs += triple + [plane] + side(1) + [own, pl.BlockSpec(memory_space=pl.ANY)]
    levels = pl.BlockSpec((slab + 1, tile, lanes), lambda i, p: (0, i, 0))
    shape = (slab, width, lanes)
    return pl.pallas_call(
        old_image_kernel,
        grid_spec=pltpu.PrefetchScalarGridSpec(
            num_scalar_prefetch=1,
            grid=(width // tile,),
            in_specs=specs,
            out_specs=[own, fixed((1, 1, 128)), plane, levels, own, fixed((slab, 8, lanes)), own],
            scratch_shapes=[pltpu.VMEM((slab + 1, tile + 16, lanes), F32)] * 2
            + [pltpu.VMEM((slab, 8, lanes), F32), pltpu.VMEM((2, 8, lanes), F32)],
        ),
        out_shape=[
            hbm(shape),
            jax.ShapeDtypeStruct((1, 1, 128), F32),
            hbm((1, width, lanes)),
            hbm((slab + 1, width, lanes)),
            hbm(shape),
            hbm((slab, 8, lanes)),
            hbm(shape),
        ],
        compiler_params=params(32),
        cost_estimate=cost(100 * slab * width * lanes, 8 * slab * width * lanes),
        name="old_image",
    )(
        place, density, direction, direction, direction, *belows, *sides,
        fraction, fraction, fraction, fraction_below, *sides, residual, order,
    )


def new_image_kernel(
    low_ref, low_next, high_ref, high_next, lo_ref, hi_ref, z_ref, x_ref, x_first_ref, y_ref,
    residual_ref, old_ref, face_ref, kept_ref, image_ref, out_sums_ref, field, before_ref, sums_ref,
):
    slab, tile, lanes = image_ref.shape
    step, steps = pl.program_id(0), pl.num_programs(0)
    own = slice(8, 8 + tile)
    field[0:2, own] = low_ref[...]
    field[2:, own] = high_ref[...]

    @pl.when(step == 0)
    def _():
        field[1:, 7:8] = field[1:, 8:9] + lo_ref[...]
        sums_ref[...] = jnp.zeros_like(sums_ref)
        for level in range(slab):
            mid = field[level + 1, 0:8]
            drop = mid - next_row(field[level + 1, 8:16], mid)
            row_ids = lax.broadcasted_iota(jnp.int32, mid.shape, 0)
            flux = jnp.where(row_ids == 7, x_first_ref[level] * drop, 0.0)
            before_ref[level] = pltpu.roll(flux, 1, 0)

    @pl.when(step == steps - 1)
    def _():
        field[1:, 8 + tile : 9 + tile] = field[1:, 7 + tile : 8 + tile] - hi_ref[...]

    @pl.when(step < steps - 1)
    def _():
        field[1:2, 8 + tile : 9 + tile] = low_next[1:2, 0:1]
        field[2:, 8 + tile : 9 + tile] = high_next[:, 0:1]

    def rows(i, carry):
        at = pl.multiple_of(8 + 8 * i, 8)
        here = pl.ds(at, 8)
        own = pl.ds(pl.multiple_of(8 * i, 8), 8)
        mid, up = field[0, here], field[1, here]
        above = z_ref[0, own] * (mid - up)
        totals = [mid * above, jnp.zeros((8, lanes), F32), mid * face_ref[0, own]]
        for level in range(slab):
            below, mid = above, up
            if level < slab - 1:
                up = field[level + 2, here]
                above = z_ref[level + 1, own] * (mid - up)
            else:
                above = z_ref[slab, own] * mid
            after = x_ref[level, own] * (mid - next_row(field[level + 1, pl.ds(at + 8, 8)], mid))
            before = previous_row(before_ref, level, after)
            right = y_ref[level, own] * (mid - pltpu.roll(mid, lanes - 1, 1))
            image = (above - below) + (after - before) + (right - pltpu.roll(right, 1, 1))
            image_ref[level, own] = image
            totals[0] = totals[0] + mid * image
            totals[1] = totals[1] + mid * residual_ref[level, own]
            totals[2] = totals[2] + mid * old_ref[level, own]
        for k in range(3):
            sums_ref[k] += totals[k]
        return carry

    lax.fori_loop(0, tile // 8, rows, 0)

    @pl.when(step == steps - 1)
    def _():
        pack_sums(out_sums_ref, kept_ref[0], 2, sums_ref)


def new_image(low, high, jump_rows, coefficients, residual, image_old, old_face, sums_old, copies):
    slab, width, lanes = residual.shape
    tile = stencil_tile(width)
    per = tile // 8
    last = width // 8 - 1

    def pair(levels):
        return [
            pl.BlockSpec((levels, tile, lanes), lambda i: (0, i, 0)),
            pl.BlockSpec((levels, 8, lanes), lambda i: (0, jnp.minimum((i + 1) * per, last), 0)),
        ]

    def side(k):
        return pl.BlockSpec((slab, 1, lanes), lambda i: (k, 0, 0))

    own = pl.BlockSpec((slab, tile, lanes), lambda i: (0, i, 0))
    plane = pl.BlockSpec((1, tile, lanes), lambda i: (0, i, 0))
    levels = pl.BlockSpec((slab + 1, tile, lanes), lambda i: (0, i, 0))
    specs = pair(2) + pair(slab - 1) + [side(0), side(1), levels, own, fixed((slab, 8, lanes)), own]
    specs += [own, own, plane, fixed((1, 1, 128))]
    low, high = in_hbm(low), in_hbm(high)
    return pl.pallas_call(
        new_image_kernel,
        grid=(width // tile,),
        in_specs=specs,
        out_specs=[own, fixed((copies, 1, 128))],
        scratch_shapes=[
            pltpu.VMEM((slab + 1, tile + 16, lanes), F32),
            pltpu.VMEM((slab, 8, lanes), F32),
            pltpu.VMEM((3, 8, lanes), F32),
        ],
        out_shape=[hbm((slab, width, lanes)), jax.ShapeDtypeStruct((copies, 1, 128), F32)],
        compiler_params=params(32),
        cost_estimate=cost(40 * slab * width * lanes, 8 * slab * width * lanes),
        name="new_image",
    )(
        low, low, high, high, jump_rows, jump_rows, *[in_hbm(c) for c in coefficients],
        in_hbm(residual), in_hbm(image_old), in_hbm(old_face), sums_old,
    )


def update_kernel(sums_ref, low_ref, high_ref, direction_ref, solution_ref, residual_ref, old_ref, new_ref, old_face_ref, new_face_ref, *refs):
    solution_out, residual_out, direction_out = refs
    slab, _, lanes = direction_ref.shape
    packed = jnp.sum(sums_ref[...], axis=0)
    group_ids = lax.broadcasted_iota(jnp.int32, (1, 128), 1) // 16
    t0, t3, t4, t2, t1 = (
        jnp.broadcast_to(
            jnp.sum(jnp.where(group_ids == k, packed, 0.0), axis=1, keepdims=True), (1, 128)
        )
        for k in range(5)
    )
    t5 = t1
    conjugate = -t1 / t0
    along_r = t2 + conjugate * t3
    curvature = t4 + conjugate * (t1 + t5) + conjugate * conjugate * t0
    step_len = along_r / curvature
    conjugate = jnp.concatenate([conjugate] * (lanes // 128), axis=1)
    step_len = jnp.concatenate([step_len] * (lanes // 128), axis=1)
    for level in range(slab):
        precond = high_ref[level - 1] if level else low_ref[0]
        turned = precond + conjugate * direction_ref[level]
        direction_out[level] = turned
        solution_out[level] = solution_ref[level] + step_len * turned
        image = new_ref[level] + conjugate * old_ref[level]
        if level == slab - 1:
            image = image + (new_face_ref[0] + conjugate * old_face_ref[0])
        residual_out[level] = residual_ref[level] - step_len * image


def update(sums, precond_low, precond_high, direction, solution, residual, image_old, image_new, old_face, new_face):
    slab, width, lanes = direction.shape
    tile = divisor_of(width, 8, 24)
    own = pl.BlockSpec((slab, tile, lanes), lambda i: (0, i, 0))
    return pl.pallas_call(
        update_kernel,
        grid=(width // tile,),
        in_specs=[
            fixed(sums.shape),
            pl.BlockSpec((1, tile, lanes), lambda i: (1, i, 0)),
            pl.BlockSpec((slab - 1, tile, lanes), lambda i: (0, i, 0)),
        ]
        + [own] * 5
        + [pl.BlockSpec((1, tile, lanes), lambda i: (0, i, 0))] * 2,
        out_specs=[own] * 3,
        out_shape=[jax.ShapeDtypeStruct(direction.shape, F32)] * 3,
        compiler_params=params(28),
        cost_estimate=cost(10 * direction.size, 10 * direction.size),
        name="update",
    )(
        sums, in_hbm(precond_low), in_hbm(precond_high), in_hbm(direction), in_hbm(solution), in_hbm(residual),
        in_hbm(image_old), in_hbm(image_new), old_face, new_face,
    )


def body(solution, residual, direction, volume_fraction, density):
    slab, width, length = residual.shape
    groups, plane_parts = lax.axis_size("gz"), lax.axis_size("xy")
    half = groups // 2
    me, here = lax.axis_index("gz"), lax.axis_index("xy")
    upper = me >= half
    rank = jnp.where(upper, groups - 1 - me, me)
    innermost = rank == half - 1
    flags = [me, here, here == 0, here == plane_parts - 1, upper, innermost, me == 0, me == groups - 1]
    place = jnp.stack(flags + [rank]).astype(jnp.int32)
    scale = (2.0 / (1.0 / density[0] + 1.0 / density[1])).reshape(1)

    up, down = neighbours(groups)
    left, right = neighbours(plane_parts)[::-1]
    top, fraction_top, first_rows, last_rows = cut_borders(direction, volume_fraction)
    fraction_below = lax.ppermute(fraction_top, "gz", up)
    below = lax.ppermute(top, "gz", up[1:]) if up[1:] else jnp.zeros_like(top)
    sides = (lax.ppermute(last_rows, "xy", right), lax.ppermute(first_rows, "xy", left))

    spectral = forward_rows(residual.reshape(slab * width, length), scale)
    spectral = spectral.reshape(slab, width, length)
    ratios = pivots(width, length, slab, groups, place)
    inward = [[(s - 1, s), (groups - s, groups - 1 - s)] for s in range(1, half)]
    outward = [[(j, i) for i, j in pairs] for pairs in reversed(inward)]
    across = [(half - 1, half), (half, half - 1)]
    parts = end_responses(spectral, place, groups)
    modes, last, outer, through = eliminate(spectral, ratios, (fraction_below, parts), place)
    zero = jnp.zeros_like(last)
    ends = jnp.sum(lax.all_to_all(parts, "gz", 0, 0, tiled=True), axis=0)
    late_top, ends = lax.optimization_barrier((top, ends))
    below_too = lax.ppermute(late_top, "gz", up[:1])
    all_ends = lax.all_to_all(
        jnp.broadcast_to(ends[None], (plane_parts,) + ends.shape), "xy", 0, 0, tiled=True
    )
    levels_jump = jumps(all_ends, place, width, groups)
    all_jumps = lax.all_to_all(levels_jump, "gz", 0, 0, tiled=True)
    incoming, mine = zero, last
    for k, pairs in enumerate(inward):
        arrived = lax.ppermute(mine, "gz", pairs)
        incoming = incoming + arrived if k else arrived
        mine = relay(last, through, incoming, (below, levels_jump) + sides)
    theirs = lax.ppermute(mine, "gz", across)
    message, following = turn(mine, theirs, incoming, outer, zero, ratios, (below_too,), place, 0)
    back = zero
    for k, pairs in enumerate(outward):
        if k:
            message, following = turn(
                mine, theirs, incoming, outer, following + back, ratios, (below_too,), place, 0
            )
        back = lax.ppermute(message, "gz", pairs)

    image_old, sums_old, old_face, *coefficients = old_image(
        in_hbm(direction), (below, below_too), sides, in_hbm(volume_fraction), fraction_below,
        density, in_hbm(residual), message, place
    )
    old_above = lax.ppermute(old_face, "gz", down)
    jumped = border_solve(all_jumps, message, place, width, length, slab)
    solved = substitute(modes, ratios, incoming, following, back, jumped, sums_old, place)
    precond_low, precond_high, jump_rows, new_face = inverse_rows(
        solved.reshape((slab + 1) * width, length), all_jumps, fraction_below,
        in_hbm(volume_fraction), density, place, width
    )
    new_above = lax.ppermute(new_face, "gz", down)
    image_new, sums = new_image(
        precond_low, precond_high, jump_rows, coefficients, residual, image_old, old_face, sums_old,
        groups * plane_parts
    )
    gathered = lax.all_to_all(sums, ("gz", "xy"), 0, 0, tiled=True)
    new_solution, new_residual, new_direction = update(
        gathered, precond_low, precond_high, direction, solution, residual, image_old, image_new,
        old_above, new_above
    )
    return (new_solution, new_residual, new_direction)


def solution(mesh):
    placed = P("gz", "xy", None)
    return jax.shard_map(
        body,
        mesh=mesh,
        in_specs=(placed, placed, placed, placed, P()),
        out_specs=(placed, placed, placed),
        check_vma=False,
    )
```
